128 devices in a mesh: grid: 2 (over y_hi), colat: 8 (over x, core), lon: 8 (over z, y_lo).
Axes of the slice: x: 4, y: 4 (y_hi: 2, y_lo: 2; y = y_hi * 2 + y_lo), z: 4, core: 2. Of those that a mesh axis runs over, the one named last changes fastest.
Arguments:
- state: float32 [2, 8, 64, 64, 3072], P('grid', None, None, 'colat', 'lon'), may hold values from -6 to 6
- section: float32 [2, 8, 64, 64, 3072], P('grid', None, None, 'colat', 'lon'), may hold values from -6 to 6
- diffusivity: float32 [8], replicated, may hold values from 0.2 to 0.8
- coupling: float32 [8, 8], replicated, may hold values from -2 to 2
- pairs: int32 [2, 8, 8, 784], P('grid', 'colat', 'lon'), may hold values from 0 to 2686, as said below
- fractions: float32 [2, 8, 8, 2, 784], P('grid', 'colat', 'lon'), may hold values from 0 to 1
Outputs:
- new_state: float32 [2, 8, 64, 64, 3072], P('grid', None, None, 'colat', 'lon')
- new_section: float32 [2, 8, 64, 64, 3072], P('grid', None, None, 'colat', 'lon')
The draws below stay inside these ranges and needn't reach their ends.
Inputs may be any that keep to these rules, and one draw needn't show every extreme that they name: `pairs`: q = row * 384 + column with row below 7 and column below 383, so that the 2 x 2 block q, q + 1, q + 384, q + 385 lies in the matched tile. Only tiles on a grid's edge use their strips, as the border layout says; other slots are never read.
All inputs are finite; a program needn't handle non-finite values.
Results may differ from the reference program's by a relative error of at most 0.0001.
Values sent between devices are 32-bit elements; how exact they have to be, the bound alone decides.
No kernel may reach another device: no remote copies, remote signals or barrier semaphores. Data moves between devices by JAX's collectives and lax.ppermute only.
A program may use at most 192 MiB of HBM per device.

```python
import math
import jax
import jax.numpy as jnp
from jax import lax

FIELDS = 8
R = 64
CT = 8
LT = 384
CTILES = 8
LTILES = 8
NCOL = 64
NLON = 3072
RIM = 784


def draw_pairs(key, part):
    key = jax.random.fold_in(key, 7)
    key_rows, key_cols = jax.random.split(key)
    rows = jax.random.randint(key_rows, (2, CTILES, LTILES, RIM), 0, CT - 1)
    cols = jax.random.randint(key_cols, (2, CTILES, LTILES, RIM), 0, LT - 1)
    corner = rows * LT + cols
    corner = corner.at[..., 0].set(0)
    corner = corner.at[..., 1].set(CT * LT - LT - 2)
    return corner.astype(jnp.int32)


def block_scale(rng, dims, cuts, smallest, largest):
    def one(dim, blocks):
        heights = jax.random.uniform(jax.random.fold_in(jax.random.fold_in(rng, 6), dim), (blocks,), jnp.float32, smallest / len(cuts), largest / len(cuts))
        return jnp.repeat(jnp.exp(heights), dims[dim] // blocks).reshape((-1,) + (1,) * (len(dims) - dim - 1))

    loudness = one(*cuts[0])
    for cut in cuts[1:]:
        loudness = loudness * one(*cut)
    return loudness


def noise(stream_key, shape, deviation, reach, cuts=(), kind=jnp.bfloat16):
    gain = block_scale(stream_key, shape, cuts, -0.22, 0.18) if cuts else 1.0
    entries = jax.random.normal(stream_key, shape, jnp.float32) * deviation * gain
    return jnp.minimum(jnp.maximum(entries, -reach), reach).astype(kind)


def setup_inputs(seed: int = 0) -> dict:
    keys = jax.random.split(jax.random.key(seed), 7)
    return {
        "state": noise(keys[0], (2, FIELDS, R, NCOL, NLON), 1.0, 6.0, ((0, 2), (3, 8), (4, 8)), jnp.float32),
        "section": noise(keys[1], (2, FIELDS, R, NCOL, NLON), 1.0, 6.0, ((0, 2), (3, 8), (4, 8)), jnp.float32),
        "diffusivity": jnp.clip(jnp.exp(jax.random.uniform(keys[2], (FIELDS,), jnp.float32, math.log(0.2), math.log(0.8))), 0.2, 0.8),
        "coupling": noise(keys[3], (FIELDS, FIELDS), FIELDS ** -0.5, 2.0, (), jnp.float32),
        "pairs": draw_pairs(jax.random.fold_in(keys[6], 71), 0),
        "fractions": jnp.clip(1.0 * jax.random.uniform(keys[5], (2, CTILES, LTILES, 2, RIM), jnp.float32) ** block_scale(keys[5], (2, CTILES, LTILES, 2, RIM), ((0, 2), (1, 8), (2, 8)), -0.2, 0.2), 0.0, 1.0),
    }


ADVECT = 0.5
TIME_STEP = 0.25
SECTION_KEEP = -5.0 / 9.0
SECTION_GAIN = 15.0 / 16.0


def window(padded, shift_r, shift_t, shift_p):
    levels = padded.shape[-3] - 4
    rows = padded.shape[-2] - 4
    cols = padded.shape[-1] - 4
    return padded[..., 2 + shift_r:2 + shift_r + levels, 2 + shift_t:2 + shift_t + rows, 2 + shift_p:2 + shift_p + cols]


def along(padded, axis, offset):
    shifts = [0, 0, 0]
    shifts[axis] = offset
    return window(padded, shifts[0], shifts[1], shifts[2])


def second_diff(padded, axis):
    return (16.0 * (along(padded, axis, 1) + along(padded, axis, -1)) - (along(padded, axis, 2) + along(padded, axis, -2)) - 30.0 * along(padded, axis, 0)) / 12.0


def first_diff(padded, axis):
    return (8.0 * (along(padded, axis, 1) - along(padded, axis, -1)) - (along(padded, axis, 2) - along(padded, axis, -2))) / 12.0


def field_operator(padded, diffuse, velocity, inv_sin, inv_sin2):
    laplace = second_diff(padded, 0) + second_diff(padded, 1) + inv_sin2 * second_diff(padded, 2)
    advect = velocity[0] * first_diff(padded, 0) + velocity[1] * first_diff(padded, 1) + velocity[2] * inv_sin * first_diff(padded, 2)
    return diffuse * laplace - ADVECT * advect


def blend(corner_a, corner_b, corner_c, corner_d, frac_row, frac_col):
    return (1.0 - frac_row) * ((1.0 - frac_col) * corner_a + frac_col * corner_b) + frac_row * ((1.0 - frac_col) * corner_c + frac_col * corner_d)


def metric(rows_global, total_rows):
    theta = math.pi / 4 + (rows_global.astype(jnp.float32) + 0.5) * (math.pi / 2) / total_rows
    inv_sin = (1.0 / jnp.sin(theta))[:, None]
    return inv_sin, inv_sin * inv_sin


def reference(state, section, diffusivity, coupling, pairs, fractions):
    inv_sin, inv_sin2 = metric(jnp.arange(NCOL, dtype=jnp.int32), NCOL)
    new_states = []
    new_sections = []
    for grid_id in range(2):
        source = state[1 - grid_id].reshape(FIELDS, R, CTILES, CT, LTILES, LT)
        source = source.transpose(0, 1, 2, 4, 3, 5).reshape(FIELDS, R, CTILES, LTILES, CT * LT)
        corner = jnp.broadcast_to(pairs[grid_id][None, None], (FIELDS, R, CTILES, LTILES, RIM))
        picks = [jnp.take_along_axis(source, corner + offset, axis=4) for offset in (0, 1, LT, LT + 1)]
        ghost = blend(picks[0], picks[1], picks[2], picks[3], fractions[grid_id, :, :, 0][None, None], fractions[grid_id, :, :, 1][None, None])
        top = ghost[:, :, 0, :, 0:2 * LT].reshape(FIELDS, R, LTILES, 2, LT).transpose(0, 1, 3, 2, 4).reshape(FIELDS, R, 2, NLON)
        bottom = ghost[:, :, CTILES - 1, :, 0:2 * LT].reshape(FIELDS, R, LTILES, 2, LT).transpose(0, 1, 3, 2, 4).reshape(FIELDS, R, 2, NLON)
        left = ghost[:, :, :, 0, 2 * LT:2 * LT + 2 * CT].reshape(FIELDS, R, NCOL, 2)
        right = ghost[:, :, :, LTILES - 1, 2 * LT:2 * LT + 2 * CT].reshape(FIELDS, R, NCOL, 2)
        fields = state[grid_id]
        padded = jnp.pad(fields, ((0, 0), (0, 0), (2, 2), (2, 2)))
        padded = padded.at[:, :, 0:2, 2:NLON + 2].set(top)
        padded = padded.at[:, :, NCOL + 2:NCOL + 4, 2:NLON + 2].set(bottom)
        padded = padded.at[:, :, 2:NCOL + 2, 0:2].set(left)
        padded = padded.at[:, :, 2:NCOL + 2, NLON + 2:NLON + 4].set(right)
        padded = jnp.pad(padded, ((0, 0), (2, 2), (0, 0), (0, 0)))
        velocity = fields[0:3]
        operator = lax.map(lambda item: field_operator(item[0], item[1], velocity, inv_sin, inv_sin2), (padded, diffusivity))
        coupled = jnp.einsum("fg,grcl->frcl", coupling, fields, precision=lax.Precision.HIGHEST)
        operator = operator + coupled
        section_next = SECTION_KEEP * section[grid_id] + TIME_STEP * operator
        new_sections.append(section_next)
        new_states.append(fields + SECTION_GAIN * section_next)
    return jnp.stack(new_states), jnp.stack(new_sections)
```

```python
import functools
import math

import jax
import jax.numpy as jnp
import numpy as np
from jax import lax
from jax.experimental import pallas as pl
from jax.experimental.pallas import tpu as pltpu
from jax.sharding import PartitionSpec as P

FIELDS = 8
R = 64
CT = 8
LT = 384
ROWS = FIELDS * R
HALF = ROWS // 2
PAIRS = CT // 2
STRIP = 2 * LT
LANES = 128
AXES = ("grid", "colat", "lon")

KEEP = -5.0 / 9.0
GAIN = 15.0 / 16.0
STEP = 0.25
D_SCALE = STEP / 12.0
V_SCALE = STEP * 0.5 / 12.0

F32 = jnp.float32
BF16 = jnp.bfloat16
ANY = pl.BlockSpec(memory_space=pl.ANY)
VM = pl.BlockSpec(memory_space=pltpu.VMEM)
SM = pl.BlockSpec(memory_space=pltpu.SMEM)
EDGE_PLANES = (0, 1, 6, 7)


def split(value):
    high = value.astype(BF16)
    return high, (value - high.astype(F32)).astype(BF16)


def wait_all(copies):
    for copy in copies:
        copy.wait()


def edge_kernel(state, low, high, sems):
    copies = [
        pltpu.make_async_copy(state.at[:, t, :], dst.at[j], sems.at[i])
        for i, (t, dst, j) in enumerate(((0, low, 0), (1, low, 1), (6, high, 0), (7, high, 1)))
    ]
    for copy in copies:
        copy.start()
    wait_all(copies)


def build_matrices(coupling, diffusivity, la, mlo, band):
    lane = lax.broadcasted_iota(jnp.int32, (R, ROWS), 1)
    away = lax.rem(lane, R) - lax.broadcasted_iota(jnp.int32, (R, ROWS), 0)
    owner = lane // R
    near = jnp.abs(away)
    second = jnp.where(near == 0, -60.0, jnp.where(near == 1, 16.0, jnp.where(near == 2, -1.0, 0.0)))
    lane8 = lax.broadcasted_iota(jnp.int32, (8, ROWS), 1) // R
    for f in range(FIELDS):
        line = jnp.zeros((8, ROWS), F32)
        for h in range(FIELDS):
            line = jnp.where(lane8 == h, STEP * coupling[f, h], line)
        line = jnp.broadcast_to(line[0:1], (R, ROWS))
        rows = jnp.where(near == 0, line, 0.0)
        rows = rows + jnp.where(owner == f, D_SCALE * diffusivity[f] * second, 0.0)
        high, rest = split(rows)
        spot = pl.ds(f * R, R)
        la[spot, 0:HALF] = high[:, 0:HALF]
        la[spot, HALF : 2 * HALF] = high[:, 0:HALF]
        la[spot, 2 * HALF : 3 * HALF] = high[:, HALF:]
        la[spot, 3 * HALF :] = high[:, HALF:]
        mlo[spot, :] = rest
    row = lax.broadcasted_iota(jnp.int32, (HALF, HALF), 0)
    col = lax.broadcasted_iota(jnp.int32, (HALF, HALF), 1)
    step = jnp.where(row // R == col // R, col - row, 9)
    first = jnp.where(step == 1, 8.0, jnp.where(step == -1, -8.0, 0.0))
    first = first - jnp.where(step == 2, 1.0, 0.0) + jnp.where(step == -2, 1.0, 0.0)
    band[...] = first.astype(BF16)


def split_kernel(coupling, diffusivity, state, hilo, first_cols, last_cols, la, mlo, band, planes, sems):
    copies = [pltpu.make_async_copy(state.at[:, t, :], planes.at[t], sems.at[t]) for t in range(CT)]
    for copy in copies:
        copy.start()
    build_matrices(coupling, diffusivity, la, mlo, band)
    lane = lax.broadcasted_iota(jnp.int32, (R, LANES), 1)
    for t in range(CT):
        copies[t].wait()

        def field(f, carry, t=t):
            block = planes[t, pl.ds(f * R, R), :]
            high, rest = split(block)
            row = (f // 4) * ROWS + lax.rem(f, 4) * R
            row = pl.multiple_of(row, R)
            cols = slice((t % 2) * LT, (t % 2 + 1) * LT)
            hilo[t // 2, pl.ds(row, R), cols] = high
            hilo[t // 2, pl.ds(row + HALF, R), cols] = rest
            spot = f * 2 * CT + 2 * t
            mine = (lane >= spot) & (lane < spot + 2)
            first_cols[...] = jnp.where(mine, pltpu.roll(block[:, 0:LANES], spot, 1), first_cols[...])
            last_cols[...] = jnp.where(
                mine, pltpu.roll(block[:, LT - LANES :], lax.rem(spot + 2, LANES), 1), last_cols[...]
            )
            return carry

        lax.fori_loop(0, FIELDS, field, 0)


def build_weights(asked, start, width, whi, wlo):
    block = min(width, 256)
    for at in range(0, width, block):
        lanes = slice(start + at, start + at + block)
        q = asked[0:1, lanes]
        a = asked[1:2, lanes]
        b = asked[2:3, lanes]
        row = ((q + 0.5) * (1.0 / LT)).astype(jnp.int32)
        col = jnp.broadcast_to(q.astype(jnp.int32) - LT * row, (16, block))
        b = jnp.broadcast_to(b, (16, block))
        rest = 1.0 - b
        spots = [
            jnp.where(row == t, 1.0 - a, jnp.where(row == t - 1, a, 0.0)) for t in range(CT)
        ]

        def chunk(i, carry):
            cell = i * 16 + lax.broadcasted_iota(jnp.int32, (16, block), 0)
            along = jnp.where(cell == col, rest, jnp.where(cell == col + 1, b, 0.0))
            for t in range(CT):
                high, low = split(along * spots[t])
                at_row = pl.multiple_of((t % 2) * LT + i * 16, 16)
                whi[t // 2, pl.ds(at_row, 16), at : at + block] = high
                wlo[t // 2, pl.ds(at_row, 16), at : at + block] = low
            return carry

        lax.fori_loop(0, LT // 16, chunk, 0)


def dot(a, b):
    return jnp.dot(a, b, preferred_element_type=F32)


def interpolate(hilo, half, whi, wlo):
    total = None
    for p in range(PAIRS):
        both = dot(hilo[p, half * ROWS : (half + 1) * ROWS, :], whi[p])
        part = both[0:HALF] + both[HALF:] + dot(hilo[p, half * ROWS : half * ROWS + HALF, :], wlo[p])
        total = part if total is None else total + part
    return total


def column_kernel(hilo, asked, out, whi, wlo):
    l = lax.axis_index("lon")

    @pl.when((l == 0) | (l == lax.axis_size("lon") - 1))
    def _():
        build_weights(asked, STRIP, LANES, whi, wlo)
        lane = lax.broadcasted_iota(jnp.int32, (R, LANES), 1)
        packed = jnp.zeros((R, LANES), F32)
        for half in range(2):
            got = interpolate(hilo, half, whi, wlo)
            for k in range(4):
                f = half * 4 + k
                mine = lane // (2 * CT) == f
                packed = jnp.where(mine, pltpu.roll(got[k * R : (k + 1) * R], f * 2 * CT, 1), packed)
        out[...] = packed


def row_kernel(half, hilo, asked, *refs):
    if half == 0:
        out, whi, wlo = refs
    else:
        whi, wlo, out = refs
    c = lax.axis_index("colat")

    @pl.when((c == 0) | (c == lax.axis_size("colat") - 1))
    def _():
        if half == 0:
            build_weights(asked, 0, STRIP, whi, wlo)
        for j in range(2):
            lanes = slice(j * LT, (j + 1) * LT)
            total = None
            for p in range(PAIRS):
                both = dot(hilo[p, half * ROWS : (half + 1) * ROWS, :], whi[p, :, lanes])
                part = both[0:HALF] + both[HALF:]
                part = part + dot(hilo[p, half * ROWS : half * ROWS + HALF, :], wlo[p, :, lanes])
                total = part if total is None else total + part
            out[j] = total


def shifted(tiles, by, edge, lane):
    count = len(tiles)
    turned = [pltpu.roll(tile, (-by) % LANES, 1) for tile in tiles]
    if by > 0:
        keep = lane < LANES - by
        following = turned[1:] + [edge]
        return [jnp.where(keep, turned[i], following[i]) for i in range(count)]
    keep = lane >= -by
    before = [edge] + turned[:-1]
    return [jnp.where(keep, turned[i], before[i]) for i in range(count)]


def main_kernel(
    diffusivity, metric, state, section, hilo, la, mlo, band, from_left, from_right, ghost_cols,
    new_state, new_section, part,
    planes, register, lin, grad, left, right, out_state, out_section, sems, reg_sems, out_sems,
):
    c = lax.axis_index("colat")
    l = lax.axis_index("lon")
    reads = [pltpu.make_async_copy(state.at[:, t, :], planes.at[t], sems.at[t]) for t in range(CT)]
    regs = [
        pltpu.make_async_copy(section.at[:, t, :], register.at[t % 4], reg_sems.at[t % 4])
        for t in range(CT)
    ]
    for t in range(CT):
        reads[t].start()
        if t < 4:
            regs[t].start()
    left[...] = jnp.where(l == 0, ghost_cols[...], from_left[...])
    right[...] = jnp.where(l == lax.axis_size("lon") - 1, ghost_cols[...], from_right[...])
    lane = lax.broadcasted_iota(jnp.int32, (16, LANES), 1)
    pending = {}
    for p in range(PAIRS):
        lin[...] = (
            dot(la[...], hilo[p])
            + dot(mlo[:, 0:HALF], hilo[p, 0:HALF, :])
            + dot(mlo[:, HALF:], hilo[p, ROWS : ROWS + HALF, :])
        )
        for half in range(2):
            base = half * ROWS
            grad[half * HALF : (half + 1) * HALF, :] = dot(band[...], hilo[p, base : base + HALF, :]) + dot(
                band[...], hilo[p, base + HALF : base + ROWS, :]
            )
        for t in (2 * p, 2 * p + 1):
            if t == 0:
                wait_all(reads[0:3])
            elif t + 2 < CT:
                reads[t + 2].wait()
            regs[t].wait()
            final = t not in EDGE_PLANES
            slot = t % 2
            if final and slot in pending:
                wait_all(pending.pop(slot))
            inv_sin = metric[c * CT + t]
            inv_sin2 = inv_sin * inv_sin
            edge_at = EDGE_PLANES.index(t) if not final else None

            def block(i, carry, t=t, final=final, slot=slot, inv_sin=inv_sin, inv_sin2=inv_sin2, edge_at=edge_at):
                f = i // 4
                r0 = pl.multiple_of(lax.rem(i, 4) * 16, 16)
                row = pl.multiple_of(i * 16, 16)
                rows = pl.ds(row, 16)
                diffuse = diffusivity[f] * D_SCALE
                spot = f * 2 * CT + 2 * t
                hl = left[pl.ds(r0, 16), :]
                hr = right[pl.ds(r0, 16), :]
                left1 = pltpu.roll(hl, lax.rem(2 * LANES - spot - 1, LANES), 1)
                left2 = pltpu.roll(hl, lax.rem(2 * LANES - spot, LANES), 1)
                right1 = pltpu.roll(hr, lax.rem(2 * LANES - 1 - spot, LANES), 1)
                right2 = pltpu.roll(hr, lax.rem(2 * LANES - 2 - spot, LANES), 1)
                tiles = [planes[t, rows, k * LANES : (k + 1) * LANES] for k in range(3)]
                plus1 = shifted(tiles, 1, right1, lane)
                plus2 = shifted(tiles, 2, right2, lane)
                minus1 = shifted(tiles, -1, left1, lane)
                minus2 = shifted(tiles, -2, left2, lane)
                for k in range(3):
                    cols = slice(k * LANES, (k + 1) * LANES)
                    wide = slice((t % 2) * LT + k * LANES, (t % 2) * LT + (k + 1) * LANES)
                    here = tiles[k]
                    vel = [planes[t, pl.ds(v * R + r0, 16), cols] * V_SCALE for v in range(3)]
                    lap_p = 16.0 * (plus1[k] + minus1[k]) - (plus2[k] + minus2[k]) - 30.0 * here
                    adv_p = 8.0 * (plus1[k] - minus1[k]) - (plus2[k] - minus2[k])
                    near = None
                    far = None
                    up1 = planes[t + 1, rows, cols] if t + 1 < CT else None
                    dn1 = planes[t - 1, rows, cols] if t >= 1 else None
                    up2 = planes[t + 2, rows, cols] if t + 2 < CT else None
                    dn2 = planes[t - 2, rows, cols] if t >= 2 else None
                    if up1 is None:
                        near, near_d = dn1, -dn1
                    elif dn1 is None:
                        near, near_d = up1, up1
                    else:
                        near, near_d = up1 + dn1, up1 - dn1
                    if up2 is None:
                        far, far_d = dn2, -dn2
                    elif dn2 is None:
                        far, far_d = up2, up2
                    else:
                        far, far_d = up2 + dn2, up2 - dn2
                    lap = (16.0 * near - far) + inv_sin2 * lap_p
                    adv = (
                        vel[0] * grad[rows, wide]
                        + vel[1] * (8.0 * near_d - far_d)
                        + (vel[2] * inv_sin) * adv_p
                    )
                    fresh = KEEP * register[t % 4, rows, cols] + lin[rows, wide] + diffuse * lap - adv
                    if final:
                        out_section[slot, rows, cols] = fresh
                        out_state[slot, rows, cols] = here + GAIN * fresh
                    else:
                        part[edge_at, rows, cols] = fresh
                return carry

            lax.fori_loop(0, ROWS // 16, block, 0)
            if t + 4 < CT:
                regs[t + 4].start()
            if final:
                writes = [
                    pltpu.make_async_copy(out_section.at[slot], new_section.at[:, t, :], out_sems.at[slot, 0]),
                    pltpu.make_async_copy(out_state.at[slot], new_state.at[:, t, :], out_sems.at[slot, 1]),
                ]
                for copy in writes:
                    copy.start()
                pending[slot] = writes
    for writes in pending.values():
        wait_all(writes)


def finish_kernel(
    diffusivity, part, low, high, below, above, ghost0, ghost1, old_state, old_section,
    new_state, new_section, halo, out_state, out_section, sems, out_sems,
):
    del old_state, old_section
    c = lax.axis_index("colat")
    top = c == 0
    bottom = c == lax.axis_size("colat") - 1
    for side, (edge, received) in enumerate(((top, below), (bottom, above))):

        @pl.when(edge)
        def _(side=side):
            for half, ghost in enumerate((ghost0, ghost1)):
                rows = pl.ds(half * HALF, HALF)
                copy = pltpu.make_async_copy(ghost, halo.at[side, :, rows, :], sems.at[side, half])
                copy.start()
            for half, ghost in enumerate((ghost0, ghost1)):
                rows = pl.ds(half * HALF, HALF)
                pltpu.make_async_copy(ghost, halo.at[side, :, rows, :], sems.at[side, half]).wait()

        @pl.when(jnp.logical_not(edge))
        def _(side=side, received=received):
            copy = pltpu.make_async_copy(received, halo.at[side], sems.at[side, 2])
            copy.start()
            copy.wait()

    writes = []
    for i, t in enumerate(EDGE_PLANES):
        source = low if i < 2 else high
        j = i % 2
        side = i // 2

        def block(n, carry, i=i, source=source, j=j, side=side):
            f = n // 4
            rows = pl.ds(pl.multiple_of(n * 16, 16), 16)
            r0 = pl.multiple_of(R + lax.rem(n, 4) * 16, 16)
            diffuse = diffusivity[f] * D_SCALE
            vel = source[j, pl.ds(r0, 16), :] * V_SCALE
            near = halo[side, 1 - side, rows, :]
            if i in (0, 3):
                outer = halo[side, side, rows, :]
                vel = vel if i == 0 else -vel
                fix = diffuse * (16.0 * near - outer) + vel * (8.0 * near - outer)
            else:
                fix = -(diffuse + vel) * near if i == 1 else -(diffuse - vel) * near
            fresh = part[i, rows, :] + fix
            out_section[i, rows, :] = fresh
            out_state[i, rows, :] = source[j, rows, :] + GAIN * fresh
            return carry

        lax.fori_loop(0, ROWS // 16, block, 0)
        for k, (buffer, out) in enumerate(((out_section, new_section), (out_state, new_state))):
            copy = pltpu.make_async_copy(buffer.at[i], out.at[:, t, :], out_sems.at[i, k])
            copy.start()
            writes.append(copy)
    wait_all(writes)


def sds(shape, kind=F32):
    return jax.ShapeDtypeStruct(shape, kind)


def params(mib):
    return pltpu.CompilerParams(vmem_limit_bytes=mib * 2**20)


def at(g, c, l, sizes):
    return (g * sizes[1] + c) * sizes[2] + l


def local(state, section, diffusivity, coupling, pairs, fractions):
    sizes = tuple(lax.axis_size(axis) for axis in AXES)
    grids, tiles_c, tiles_l = sizes
    tiles = [(g, c, l) for g in range(grids) for c in range(tiles_c) for l in range(tiles_l)]

    def mates(chosen):
        return [(at(g, c, l, sizes), at(1 - g, c, l, sizes)) for g, c, l in tiles if chosen(c, l)]

    def on_rows(c, l):
        return c in (0, tiles_c - 1)

    def on_cols(c, l):
        return l in (0, tiles_l - 1)

    fields = state.reshape(ROWS, CT, LT)
    register = section.reshape(ROWS, CT, LT)
    request = jnp.concatenate([pairs.reshape(1, -1).astype(F32), fractions.reshape(2, -1)], axis=0)
    request = jnp.pad(request, ((0, 0), (0, STRIP + LANES - request.shape[1])))
    asked = lax.ppermute(request, AXES, mates(lambda c, l: on_rows(c, l) or on_cols(c, l)))

    plane2 = sds((2, ROWS, LT))
    low, high = pl.pallas_call(
        edge_kernel,
        out_shape=(plane2, plane2),
        in_specs=[ANY],
        out_specs=(ANY, ANY),
        scratch_shapes=[pltpu.SemaphoreType.DMA((4,))],
        compiler_params=params(4),
        name="edge_planes",
    )(fields)
    ahead = [(i, i + 1) for i in range(tiles_c - 1)]
    back = [(i + 1, i) for i in range(tiles_c - 1)]
    below = lax.ppermute(high, "colat", ahead)
    above = lax.ppermute(low, "colat", back)

    halo2 = sds((R, LANES))
    hilo, first_cols, last_cols, la, mlo, band = pl.pallas_call(
        split_kernel,
        out_shape=(
            sds((PAIRS, 2 * ROWS, 2 * LT), BF16), halo2, halo2,
            sds((ROWS, 2 * ROWS), BF16), sds((ROWS, ROWS), BF16), sds((HALF, HALF), BF16),
        ),
        in_specs=[SM, SM, ANY],
        out_specs=(VM,) * 6,
        scratch_shapes=[pltpu.VMEM((CT, ROWS, LT), F32), pltpu.SemaphoreType.DMA((CT,))],
        compiler_params=params(20),
        name="split_planes",
    )(coupling, diffusivity, fields)
    from_left = lax.ppermute(last_cols, "lon", [(i, i + 1) for i in range(tiles_l - 1)])
    from_right = lax.ppermute(first_cols, "lon", [(i + 1, i) for i in range(tiles_l - 1)])

    served_cols = pl.pallas_call(
        column_kernel,
        out_shape=halo2,
        in_specs=[VM, VM],
        out_specs=VM,
        scratch_shapes=[pltpu.VMEM((PAIRS, 2 * LT, LANES), BF16)] * 2,
        compiler_params=params(16),
        name="border_columns",
    )(hilo, asked)
    ghost_cols = lax.ppermute(served_cols, AXES, mates(on_cols))

    weights = sds((PAIRS, 2 * LT, STRIP), BF16)
    half_rows = sds((2, HALF, LT))
    served0, whi, wlo = pl.pallas_call(
        functools.partial(row_kernel, 0),
        out_shape=(half_rows, weights, weights),
        in_specs=[VM, VM],
        out_specs=(VM, VM, VM),
        compiler_params=params(24),
        name="border_rows_0",
    )(hilo, asked)
    ghost0 = lax.ppermute(served0, AXES, mates(on_rows))
    served1 = pl.pallas_call(
        functools.partial(row_kernel, 1),
        out_shape=half_rows,
        in_specs=[VM, VM, VM, VM],
        out_specs=VM,
        compiler_params=params(24),
        name="border_rows_1",
    )(hilo, asked, whi, wlo)
    ghost1 = lax.ppermute(served1, AXES, mates(on_rows))

    theta = math.pi / 4 + (np.arange(tiles_c * CT) + 0.5) * (math.pi / 2) / (tiles_c * CT)
    metric = jnp.asarray((1.0 / np.sin(theta)).astype(np.float32))
    whole = sds((ROWS, CT, LT))
    new_state, new_section, part = pl.pallas_call(
        main_kernel,
        out_shape=(whole, whole, sds((4, ROWS, LT))),
        in_specs=[SM, SM, ANY, ANY, VM, VM, VM, VM, VM, VM, VM],
        out_specs=(ANY, ANY, VM),
        scratch_shapes=[
            pltpu.VMEM((CT, ROWS, LT), F32),
            pltpu.VMEM((4, ROWS, LT), F32),
            pltpu.VMEM((ROWS, 2 * LT), F32),
            pltpu.VMEM((ROWS, 2 * LT), F32),
            pltpu.VMEM((R, LANES), F32),
            pltpu.VMEM((R, LANES), F32),
            pltpu.VMEM((2, ROWS, LT), F32),
            pltpu.VMEM((2, ROWS, LT), F32),
            pltpu.SemaphoreType.DMA((CT,)),
            pltpu.SemaphoreType.DMA((4,)),
            pltpu.SemaphoreType.DMA((2, 2)),
        ],
        compiler_params=params(34),
        name="interior",
    )(diffusivity, metric, fields, register, hilo, la, mlo, band, from_left, from_right, ghost_cols)

    new_state, new_section = pl.pallas_call(
        finish_kernel,
        out_shape=(whole, whole),
        in_specs=[SM, VM, VM, VM, ANY, ANY, ANY, ANY, ANY, ANY],
        out_specs=(ANY, ANY),
        scratch_shapes=[
            pltpu.VMEM((2, 2, ROWS, LT), F32),
            pltpu.VMEM((4, ROWS, LT), F32),
            pltpu.VMEM((4, ROWS, LT), F32),
            pltpu.SemaphoreType.DMA((2, 3)),
            pltpu.SemaphoreType.DMA((4, 2)),
        ],
        input_output_aliases={8: 0, 9: 1},
        compiler_params=params(30),
        name="finish_edges",
    )(diffusivity, part, low, high, below, above, ghost0, ghost1, new_state, new_section)
    return new_state.reshape(state.shape), new_section.reshape(section.shape)


def solution(mesh):
    field = P("grid", None, None, "colat", "lon")
    placed = (field, field, P(), P(), P("grid", "colat", "lon", None), P("grid", "colat", "lon", None, None))
    return jax.shard_map(
        local, mesh=mesh, in_specs=placed, out_specs=(field, field), check_vma=False
    )
```

```python
import functools
import math

import jax
import jax.numpy as jnp
import numpy as np
from jax import lax
from jax.experimental import pallas as pl
from jax.experimental.pallas import tpu as pltpu
from jax.sharding import PartitionSpec as P

FIELDS = 8
R = 64
CT = 8
LT = 384
ROWS = FIELDS * R
HALF = ROWS // 2
PAIRS = CT // 2
STRIP = 2 * LT
LANES = 128
AXES = ("grid", "colat", "lon")

KEEP = -5.0 / 9.0
GAIN = 15.0 / 16.0
STEP = 0.25
D_SCALE = STEP / 12.0
V_SCALE = STEP * 0.5 / 12.0

F32 = jnp.float32
BF16 = jnp.bfloat16
ANY = pl.BlockSpec(memory_space=pl.ANY)
VM = pl.BlockSpec(memory_space=pltpu.VMEM)
SM = pl.BlockSpec(memory_space=pltpu.SMEM)
EDGE_PLANES = (0, 1, 6, 7)
SEAM = 32
FIRST = {1: 8.0, -1: -8.0, 2: -1.0, -2: 1.0}
SECOND = {0: -30.0, 1: 16.0, -1: 16.0, 2: -1.0, -2: -1.0}


def longitude_bands():
    fixed = np.zeros((3, 2 * LANES, 2 * LANES), np.float32)
    halo = np.zeros((2, CT, 32, 2 * LANES), np.float32)
    for k in range(3):
        for n in range(LANES):
            for base, stencil in ((0, FIRST), (LANES, SECOND)):
                for offset, value in stencil.items():
                    y = k * LANES + n + offset
                    if y < 0:
                        for t in range(CT):
                            halo[0, t, 2 * t + y + 2, base + n] = value
                    elif y >= LT:
                        for t in range(CT):
                            halo[1, t, 2 * CT + 2 * t + y - LT, base + n] = value
                    elif y // LANES == k:
                        fixed[k, y - k * LANES, base + n] = value
                    else:
                        lane = SEAM + y - 126 if y < LANES + 2 else SEAM + 4 + y - 254
                        fixed[k, LANES + lane, base + n] = value
    return fixed, halo


def split(value):
    high = value.astype(BF16)
    return high, (value - high.astype(F32)).astype(BF16)


def wait_all(copies):
    for copy in copies:
        copy.wait()


def build_matrices(coupling, diffusivity, la, mlo, band):
    lane = lax.broadcasted_iota(jnp.int32, (R, ROWS), 1)
    away = (lane & (R - 1)) - lax.broadcasted_iota(jnp.int32, (R, ROWS), 0)
    owner = lane >> 6
    near = jnp.abs(away)
    second = jnp.where(near == 0, -60.0, jnp.where(near == 1, 16.0, jnp.where(near == 2, -1.0, 0.0)))
    lane8 = lax.broadcasted_iota(jnp.int32, (8, ROWS), 1) >> 6
    for f in range(FIELDS):
        line = jnp.zeros((8, ROWS), F32)
        for h in range(FIELDS):
            line = jnp.where(lane8 == h, STEP * coupling[f, h], line)
        line = jnp.broadcast_to(line[0:1], (R, ROWS))
        rows = jnp.where(near == 0, line, 0.0)
        rows = rows + jnp.where(owner == f, D_SCALE * diffusivity[f] * second, 0.0)
        high, rest = split(rows)
        spot = pl.ds(f * R, R)
        la[spot, 0:HALF] = high[:, 0:HALF]
        la[spot, HALF : 2 * HALF] = high[:, 0:HALF]
        la[spot, 2 * HALF : 3 * HALF] = high[:, HALF:]
        la[spot, 3 * HALF :] = high[:, HALF:]
        mlo[spot, :] = rest
    row = lax.broadcasted_iota(jnp.int32, (HALF, HALF), 0)
    col = lax.broadcasted_iota(jnp.int32, (HALF, HALF), 1)
    step = jnp.where((row >> 6) == (col >> 6), col - row, 9)
    first = jnp.where(step == 1, 8.0, jnp.where(step == -1, -8.0, 0.0))
    first = first - jnp.where(step == 2, 1.0, 0.0) + jnp.where(step == -2, 1.0, 0.0)
    band[:, 0:HALF] = first.astype(BF16)
    band[:, HALF:] = first.astype(BF16)


def prepare_kernel(
    coupling, diffusivity, state, across, inside, hilo, borders, first_cols, last_cols, la, mlo, band,
    planes, sems, send_sems,
):
    order = (0, 1, 6, 7, 2, 3, 4, 5)
    even = lax.rem(lax.axis_index("colat"), 2) == 0

    def sends(low_to, high_to):
        return [
            pltpu.make_async_copy(planes.at[0:2], low_to, send_sems.at[0]),
            pltpu.make_async_copy(planes.at[6:8], high_to, send_sems.at[1]),
        ]

    reads = {t: pltpu.make_async_copy(state.at[:, t, :], planes.at[t], sems.at[t]) for t in order}
    for t in order:
        reads[t].start()
    build_matrices(coupling, diffusivity, la, mlo, band)
    for t in EDGE_PLANES:
        reads[t].wait()

    @pl.when(even)
    def _():
        for copy in sends(across, inside):
            copy.start()

    @pl.when(jnp.logical_not(even))
    def _():
        for copy in sends(inside, across):
            copy.start()

    lane = lax.broadcasted_iota(jnp.int32, (R, LANES), 1)
    for t in order:
        if t not in EDGE_PLANES:
            reads[t].wait()

        def field(f, carry, t=t):
            block = planes[t, pl.ds(pl.multiple_of(f * R, R), R), :]
            high, rest = split(block)
            row = pl.multiple_of(f * R + (f >> 2) * HALF, R)
            cols = slice((t % 2) * LT, (t % 2 + 1) * LT)
            hilo[t // 2, pl.ds(row, R), cols] = high
            hilo[t // 2, pl.ds(row + HALF, R), cols] = rest
            tile0, tile1, tile2 = (block[:, k * LANES : (k + 1) * LANES] for k in range(3))
            seam0 = pltpu.roll(jnp.where(lane >= 64, tile0, tile1), SEAM + 2, 1)
            seam1 = pltpu.roll(jnp.where(lane >= 64, tile1, tile2), SEAM + 6, 1)
            seam = jnp.where(lane < SEAM + 4, seam0, seam1)
            seam = jnp.where((lane >= SEAM) & (lane < SEAM + 8), seam, 0.0)
            high, rest = split(seam)
            borders[t, pl.ds(row, R), :] = high
            borders[t, pl.ds(row + HALF, R), :] = rest
            spot = f * 2 * CT + 2 * t
            ends = pltpu.roll(jnp.where(lane < 64, tile0, tile2), spot, 1)
            first_cols[...] = jnp.where((lane >= spot) & (lane < spot + 2), ends, first_cols[...])
            before = (spot + LANES - 2) & (LANES - 1)
            last_cols[...] = jnp.where((lane >= before) & (lane < before + 2), ends, last_cols[...])
            return carry

        lax.fori_loop(0, FIELDS, field, 0, unroll=4)
    for copy in sends(across, inside):
        copy.wait()


def build_weights(asked, start, width, whi, wlo):
    block = min(width, 256)
    for at in range(0, width, block):
        lanes = slice(start + at, start + at + block)
        q = asked[0:1, lanes]
        a = asked[1:2, lanes]
        b = asked[2:3, lanes]
        row = ((q + 0.5) * (1.0 / LT)).astype(jnp.int32)
        col = jnp.broadcast_to(q.astype(jnp.int32) - LT * row, (16, block))
        b = jnp.broadcast_to(b, (16, block))
        rest = 1.0 - b
        spots = [
            jnp.where(row == t, 1.0 - a, jnp.where(row == t - 1, a, 0.0)) for t in range(CT)
        ]

        def chunk(i, carry):
            cell = i * 16 + lax.broadcasted_iota(jnp.int32, (16, block), 0)
            along = jnp.where(cell == col, rest, jnp.where(cell == col + 1, b, 0.0))
            for t in range(CT):
                high, low = split(along * spots[t])
                at_row = pl.multiple_of((t % 2) * LT + i * 16, 16)
                whi[t // 2, pl.ds(at_row, 16), at : at + block] = high
                wlo[t // 2, pl.ds(at_row, 16), at : at + block] = low
            return carry

        lax.fori_loop(0, LT // 16, chunk, 0)


def dot(a, b):
    return jnp.dot(a, b, preferred_element_type=F32)


def interpolate(hilo, half, whi, wlo):
    total = None
    for p in range(PAIRS):
        both = dot(hilo[p, half * ROWS : (half + 1) * ROWS, :], whi[p])
        part = both[0:HALF] + both[HALF:] + dot(hilo[p, half * ROWS : half * ROWS + HALF, :], wlo[p])
        total = part if total is None else total + part
    return total


def column_kernel(hilo, asked, out, whi, wlo):
    l = lax.axis_index("lon")

    @pl.when((l == 0) | (l == lax.axis_size("lon") - 1))
    def _():
        build_weights(asked, STRIP, LANES, whi, wlo)
        lane = lax.broadcasted_iota(jnp.int32, (R, LANES), 1)
        packed = jnp.zeros((R, LANES), F32)
        for half in range(2):
            got = interpolate(hilo, half, whi, wlo)
            for k in range(4):
                f = half * 4 + k
                mine = (lane >> 4) == f
                packed = jnp.where(mine, pltpu.roll(got[k * R : (k + 1) * R], f * 2 * CT, 1), packed)
        out[...] = packed


def row_kernel(hilo, asked, out, whi, wlo):
    c = lax.axis_index("colat")

    @pl.when((c == 0) | (c == lax.axis_size("colat") - 1))
    def _():
        build_weights(asked, 0, STRIP, whi, wlo)
        for half in range(2):
            got = interpolate(hilo, half, whi, wlo)
            rows = slice(half * HALF, (half + 1) * HALF)
            out[0, rows, :] = got[:, 0:LT]
            out[1, rows, :] = got[:, LT:]


def main_kernel(
    diffusivity, metric, state, section, hilo, borders, la, mlo, band, fixed, halo_rows, from_left, from_right,
    ghost_cols, new_state, new_section, part,
    planes, register, lin, grad, slope, halo, bands, out_state, out_section, sems, reg_sems, out_sems,
):
    c = lax.axis_index("colat")
    l = lax.axis_index("lon")
    order = (1, 2, 0, 3)
    regs = [pltpu.make_async_copy(section.at[:, t, :], register.at[t], reg_sems.at[t]) for t in range(CT)]
    reads = [pltpu.make_async_copy(state.at[:, t, :], planes.at[t], sems.at[t]) for t in range(CT)]
    for copy in reads[0:6]:
        copy.start()
    for p in order:
        regs[2 * p].start()
        regs[2 * p + 1].start()
        if p == 1:
            reads[6].start()
            reads[7].start()
    bands[:, 0 : 2 * LANES, :] = fixed[...]
    bands[:, 2 * LANES :, :] = fixed[...]
    ghost = ghost_cols[...]
    left = jnp.where(l == 0, ghost, pltpu.roll(from_left[...], 2, 1))
    right = jnp.where(l == lax.axis_size("lon") - 1, ghost, from_right[...])
    lane = lax.broadcasted_iota(jnp.int32, (R, LANES), 1)
    for f in range(FIELDS):
        turn = f * 2 * CT
        tile = jnp.where(
            lane < 2 * CT, pltpu.roll(left, (-turn) % LANES, 1), pltpu.roll(right, (2 * CT - turn) % LANES, 1)
        )
        high, rest = split(jnp.where(lane < SEAM, tile, 0.0))
        row = (f // 4) * ROWS + (f % 4) * R
        halo[row : row + R, :] = high
        halo[row + HALF : row + HALF + R, :] = rest
    pending = {}
    scales = [diffusivity[f] * D_SCALE for f in range(FIELDS)]
    for p in order:
        lin[...] = (
            dot(la[...], hilo[p])
            + dot(mlo[:, 0:HALF], hilo[p, 0:HALF, :])
            + dot(mlo[:, HALF:], hilo[p, ROWS : ROWS + HALF, :])
        )
        for half in range(2):
            base = half * ROWS
            grad[half * HALF : (half + 1) * HALF, :] = dot(band[...], hilo[p, base : base + ROWS, :])
        for t in (2 * p, 2 * p + 1):
            for k, side in ((0, 0), (2, 1)):
                for again in range(2):
                    at_row = again * 2 * LANES + LANES
                    bands[k, at_row : at_row + 32, :] = halo_rows[side, t]
            for half in range(2):
                base = half * ROWS
                high = slice(base, base + HALF)
                rest = slice(base + HALF, base + ROWS)
                edge_high = borders[t, high, :] + halo[high, :]
                edge_rest = borders[t, rest, :] + halo[rest, :]
                for k in range(3):
                    cols = slice((t % 2) * LT + k * LANES, (t % 2) * LT + (k + 1) * LANES)
                    wide = jnp.concatenate(
                        [hilo[p, high, cols], edge_high, hilo[p, rest, cols], edge_rest], axis=1
                    )
                    slope[t % 2, half * HALF : (half + 1) * HALF, 2 * k * LANES : 2 * (k + 1) * LANES] = dot(
                        wide, bands[k]
                    )
        both = (2 * p, 2 * p + 1)
        final = p in (1, 2)
        if p == order[0]:
            wait_all(reads[0:6])
        elif p == order[1]:
            wait_all(reads[6:])
        for t in both:
            regs[t].wait()
            if final and t % 2 in pending:
                wait_all(pending.pop(t % 2))
        inv_sin = [metric[c * CT + t] for t in both]
        inv_sin2 = [value * value for value in inv_sin]

        def block(i, carry, both=both, final=final, inv_sin=inv_sin, inv_sin2=inv_sin2):
            r0 = pl.multiple_of(i * 8, 8)
            for k in range(3):
                cols = slice(k * LANES, (k + 1) * LANES)
                d1 = slice(2 * k * LANES, (2 * k + 1) * LANES)
                d2 = slice((2 * k + 1) * LANES, (2 * k + 2) * LANES)
                vels = [[planes[t, pl.ds(v * R + r0, 8), cols] * V_SCALE for v in range(3)] for t in both]
                for n in range(2):
                    vels[n][2] = vels[n][2] * inv_sin[n]
                for f in range(FIELDS):
                    rows = pl.ds(f * R + r0, 8)
                    near_by = {t: planes[t, rows, cols] for t in range(both[0] - 2, both[1] + 3) if 0 <= t < CT}
                    for n, t in enumerate(both):
                        wide = slice(n * LT + k * LANES, n * LT + (k + 1) * LANES)
                        up1, dn1, up2, dn2 = (near_by.get(t + step) for step in (1, -1, 2, -2))
                        if up1 is None:
                            near, near_d = dn1, -dn1
                        elif dn1 is None:
                            near, near_d = up1, up1
                        else:
                            near, near_d = up1 + dn1, up1 - dn1
                        if up2 is None:
                            far, far_d = dn2, -dn2
                        elif dn2 is None:
                            far, far_d = up2, up2
                        else:
                            far, far_d = up2 + dn2, up2 - dn2
                        lap = (16.0 * near - far) + inv_sin2[n] * slope[n, rows, d2]
                        adv = (
                            vels[n][0] * grad[rows, wide]
                            + vels[n][1] * (8.0 * near_d - far_d)
                            + vels[n][2] * slope[n, rows, d1]
                        )
                        fresh = (KEEP * register[t, rows, cols] + lin[rows, wide]) + (scales[f] * lap - adv)
                        if final:
                            out_section[n, rows, cols] = fresh
                            out_state[n, rows, cols] = near_by[t] + GAIN * fresh
                        else:
                            part[EDGE_PLANES.index(t), rows, cols] = fresh
            return carry

        lax.fori_loop(0, R // 8, block, 0)
        if final:
            for t in both:
                slot = t % 2
                pending[slot] = [
                    pltpu.make_async_copy(out_section.at[slot], new_section.at[:, t, :], out_sems.at[slot, 0]),
                    pltpu.make_async_copy(out_state.at[slot], new_state.at[:, t, :], out_sems.at[slot, 1]),
                ]
                for copy in pending[slot]:
                    copy.start()
    for writes in pending.values():
        wait_all(writes)


def finish_kernel(
    diffusivity, part, across, inside, from_across, from_inside, ghost, old_state, old_section,
    new_state, new_section, halo, out_state, out_section, sems, out_sems,
):
    del old_state, old_section
    c = lax.axis_index("colat")
    even = lax.rem(c, 2) == 0
    edge = (c == 0) | (c == lax.axis_size("colat") - 1)
    fill = pltpu.make_async_copy(from_across, halo, sems.at[0])
    swap = pltpu.make_async_copy(ghost, halo, sems.at[1])

    @pl.when(edge)
    def _():
        swap.start()
        swap.wait()

    @pl.when(jnp.logical_not(edge))
    def _():
        fill.start()
        fill.wait()

    def run(low, high, below, above):
        for i in range(4):
            source, received = (low, below) if i < 2 else (high, above)
            j = i % 2
            side = i // 2

            def block(n, carry, i=i, source=source, received=received, j=j, side=side):
                f = n // 4
                rows = pl.ds(pl.multiple_of(n * 16, 16), 16)
                r0 = pl.multiple_of(R + lax.rem(n, 4) * 16, 16)
                diffuse = diffusivity[f] * D_SCALE
                vel = source[j, pl.ds(r0, 16), :] * V_SCALE
                near = received[1 - side, rows, :]
                if i in (0, 3):
                    outer = received[side, rows, :]
                    vel = vel if i == 0 else -vel
                    fix = diffuse * (16.0 * near - outer) + vel * (8.0 * near - outer)
                else:
                    fix = -(diffuse + vel) * near if i == 1 else -(diffuse - vel) * near
                fresh = part[i, rows, :] + fix
                out_section[i, rows, :] = fresh
                out_state[i, rows, :] = source[j, rows, :] + GAIN * fresh
                return carry

            lax.fori_loop(0, ROWS // 16, block, 0, unroll=2)
            for copy in writes(i):
                copy.start()

    def writes(i):
        t = EDGE_PLANES[i]
        return [
            pltpu.make_async_copy(out_section.at[i], new_section.at[:, t, :], out_sems.at[i, 0]),
            pltpu.make_async_copy(out_state.at[i], new_state.at[:, t, :], out_sems.at[i, 1]),
        ]

    @pl.when(even)
    def _():
        run(across, inside, halo, from_inside)

    @pl.when(jnp.logical_not(even))
    def _():
        run(inside, across, from_inside, halo)

    for i in range(4):
        wait_all(writes(i))


def sds(shape, kind=F32):
    return jax.ShapeDtypeStruct(shape, kind)


def params(mib):
    return pltpu.CompilerParams(vmem_limit_bytes=mib * 2**20)


def cost(us):
    return pl.CostEstimate(flops=us * 10**9, bytes_accessed=us * 3 * 10**6, transcendentals=0)


def at(g, c, l, sizes):
    return (g * sizes[1] + c) * sizes[2] + l


def local(state, section, diffusivity, coupling, pairs, fractions):
    sizes = tuple(lax.axis_size(axis) for axis in AXES)
    grids, tiles_c, tiles_l = sizes
    tiles = [(g, c, l) for g in range(grids) for c in range(tiles_c) for l in range(tiles_l)]

    def mates(chosen):
        return [(at(g, c, l, sizes), at(1 - g, c, l, sizes)) for g, c, l in tiles if chosen(c, l)]

    def on_rows(c, l):
        return c in (0, tiles_c - 1)

    def on_cols(c, l):
        return l in (0, tiles_l - 1)

    fields = state.reshape(ROWS, CT, LT)
    register = section.reshape(ROWS, CT, LT)
    request = jnp.concatenate([pairs.reshape(1, -1).astype(F32), fractions.reshape(2, -1)], axis=0)
    request = jnp.pad(request, ((0, 0), (0, STRIP + LANES - request.shape[1])))
    plane2 = sds((2, ROWS, LT))
    halo2 = sds((R, LANES))
    request, fields = lax.optimization_barrier((request, fields))
    asked = lax.ppermute(request, AXES, mates(lambda c, l: on_rows(c, l) or on_cols(c, l)))
    across, inside, hilo, borders, first_cols, last_cols, la, mlo, band = pl.pallas_call(
        prepare_kernel,
        out_shape=(
            plane2, plane2, sds((PAIRS, 2 * ROWS, 2 * LT), BF16), sds((CT, 2 * ROWS, LANES), BF16), halo2, halo2,
            sds((ROWS, 2 * ROWS), BF16), sds((ROWS, ROWS), BF16), sds((HALF, ROWS), BF16),
        ),
        in_specs=[SM, SM, ANY],
        out_specs=(ANY, ANY) + (VM,) * 7,
        scratch_shapes=[
            pltpu.VMEM((CT, ROWS, LT), F32), pltpu.SemaphoreType.DMA((CT,)), pltpu.SemaphoreType.DMA((2,)),
        ],
        compiler_params=params(38),
        cost_estimate=cost(8),
        name="prepare",
    )(coupling, diffusivity, fields)
    first_cols, last_cols, asked = lax.optimization_barrier((first_cols, last_cols, asked))
    from_left = lax.ppermute(last_cols, "lon", [(i, i + 1) for i in range(tiles_l - 1)])
    from_right = lax.ppermute(first_cols, "lon", [(i + 1, i) for i in range(tiles_l - 1)])
    served_cols = pl.pallas_call(
        column_kernel,
        out_shape=halo2,
        in_specs=[VM, VM],
        out_specs=VM,
        scratch_shapes=[pltpu.VMEM((PAIRS, 2 * LT, LANES), BF16)] * 2,
        compiler_params=params(16),
        name="border_columns",
    )(hilo, asked)
    across, inside, from_left, from_right, served_cols = lax.optimization_barrier(
        (across, inside, from_left, from_right, served_cols)
    )
    ghost_cols = lax.ppermute(served_cols, AXES, mates(on_cols))
    step_across = [(i, i + 1) for i in range(1, tiles_c - 1, 2)]
    step_inside = [(i, i + 1) for i in range(0, tiles_c, 2)]
    from_across = lax.ppermute(across, "colat", step_across + [(j, i) for i, j in step_across])
    from_inside = lax.ppermute(inside, "colat", step_inside + [(j, i) for i, j in step_inside])
    hilo, served_cols = lax.optimization_barrier((hilo, served_cols))
    served = pl.pallas_call(
        row_kernel,
        out_shape=plane2,
        in_specs=[VM, VM],
        out_specs=VM,
        scratch_shapes=[pltpu.VMEM((PAIRS, 2 * LT, STRIP), BF16)] * 2,
        compiler_params=params(24),
        cost_estimate=cost(5),
        name="border_rows",
    )(hilo, asked)
    served, ghost_cols = lax.optimization_barrier((served, ghost_cols))
    ghost = lax.ppermute(served, AXES, mates(on_rows))

    theta = math.pi / 4 + (np.arange(tiles_c * CT) + 0.5) * (math.pi / 2) / (tiles_c * CT)
    metric = jnp.asarray((1.0 / np.sin(theta)).astype(np.float32))
    whole = sds((ROWS, CT, LT))
    fixed, halo_rows = (jnp.asarray(value, BF16) for value in longitude_bands())
    new_state, new_section, part = pl.pallas_call(
        main_kernel,
        out_shape=(whole, whole, sds((4, ROWS, LT))),
        in_specs=[SM, SM, ANY, ANY] + [VM] * 10,
        out_specs=(ANY, ANY, VM),
        scratch_shapes=[
            pltpu.VMEM((CT, ROWS, LT), F32),
            pltpu.VMEM((CT, ROWS, LT), F32),
            pltpu.VMEM((ROWS, 2 * LT), F32),
            pltpu.VMEM((ROWS, 2 * LT), F32),
            pltpu.VMEM((2, ROWS, 2 * LT), F32),
            pltpu.VMEM((2 * ROWS, LANES), BF16),
            pltpu.VMEM((3, 4 * LANES, 2 * LANES), BF16),
            pltpu.VMEM((2, ROWS, LT), F32),
            pltpu.VMEM((2, ROWS, LT), F32),
            pltpu.SemaphoreType.DMA((CT,)),
            pltpu.SemaphoreType.DMA((CT,)),
            pltpu.SemaphoreType.DMA((2, 2)),
        ],
        compiler_params=params(38),
        name="interior",
    )(
        diffusivity, metric, fields, register, hilo, borders, la, mlo, band, fixed, halo_rows,
        from_left, from_right, ghost_cols,
    )

    new_state, new_section = pl.pallas_call(
        finish_kernel,
        out_shape=(whole, whole),
        in_specs=[SM, VM, VM, VM, ANY, VM, ANY, ANY, ANY],
        out_specs=(ANY, ANY),
        scratch_shapes=[
            pltpu.VMEM((2, ROWS, LT), F32),
            pltpu.VMEM((4, ROWS, LT), F32),
            pltpu.VMEM((4, ROWS, LT), F32),
            pltpu.SemaphoreType.DMA((2,)),
            pltpu.SemaphoreType.DMA((4, 2)),
        ],
        input_output_aliases={7: 0, 8: 1},
        compiler_params=params(12),
        name="finish_edges",
    )(diffusivity, part, across, inside, from_across, from_inside, ghost, new_state, new_section)
    return new_state.reshape(state.shape), new_section.reshape(section.shape)


def solution(mesh):
    field = P("grid", None, None, "colat", "lon")
    placed = (field, field, P(), P(), P("grid", "colat", "lon", None), P("grid", "colat", "lon", None, None))
    return jax.shard_map(
        local, mesh=mesh, in_specs=placed, out_specs=(field, field), check_vma=False
    )
```

```python
import functools
import math

import jax
import jax.numpy as jnp
import numpy as np
from jax import lax
from jax.experimental import pallas as pl
from jax.experimental.pallas import tpu as pltpu
from jax.sharding import PartitionSpec as P

FIELDS = 8
R = 64
CT = 8
LT = 384
ROWS = FIELDS * R
HALF = ROWS // 2
PAIRS = CT // 2
STRIP = 2 * LT
LANES = 128
AXES = ("grid", "colat", "lon")

KEEP = -5.0 / 9.0
GAIN = 15.0 / 16.0
STEP = 0.25
D_SCALE = STEP / 12.0
V_SCALE = STEP * 0.5 / 12.0

F32 = jnp.float32
BF16 = jnp.bfloat16
ANY = pl.BlockSpec(memory_space=pl.ANY)
VM = pl.BlockSpec(memory_space=pltpu.VMEM)
SM = pl.BlockSpec(memory_space=pltpu.SMEM)
EDGE_PLANES = (0, 1, 6, 7)
SEAM = 32
FIRST = {1: 8.0, -1: -8.0, 2: -1.0, -2: 1.0}
SECOND = {0: -30.0, 1: 16.0, -1: 16.0, 2: -1.0, -2: -1.0}


def longitude_bands():
    fixed = np.zeros((3, 2 * LANES, 2 * LANES), np.float32)
    halo = np.zeros((2, CT, 32, 2 * LANES), np.float32)
    for k in range(3):
        for n in range(LANES):
            for base, stencil in ((0, FIRST), (LANES, SECOND)):
                for offset, value in stencil.items():
                    y = k * LANES + n + offset
                    if y < 0:
                        for t in range(CT):
                            halo[0, t, 2 * t + y + 2, base + n] = value
                    elif y >= LT:
                        for t in range(CT):
                            halo[1, t, 2 * CT + 2 * t + y - LT, base + n] = value
                    elif y // LANES == k:
                        fixed[k, y - k * LANES, base + n] = value
                    else:
                        lane = SEAM + y - 126 if y < LANES + 2 else SEAM + 4 + y - 254
                        fixed[k, LANES + lane, base + n] = value
    return fixed, halo


def split(value):
    high = value.astype(BF16)
    return high, (value - high.astype(F32)).astype(BF16)


def wait_all(copies):
    for copy in copies:
        copy.wait()


def build_matrices(coupling, diffusivity, la, mlo, band):
    lane = lax.broadcasted_iota(jnp.int32, (R, ROWS), 1)
    away = (lane & (R - 1)) - lax.broadcasted_iota(jnp.int32, (R, ROWS), 0)
    owner = lane >> 6
    near = jnp.abs(away)
    second = jnp.where(near == 0, -60.0, jnp.where(near == 1, 16.0, jnp.where(near == 2, -1.0, 0.0)))
    lane8 = lax.broadcasted_iota(jnp.int32, (8, ROWS), 1) >> 6
    for f in range(FIELDS):
        line = jnp.zeros((8, ROWS), F32)
        for h in range(FIELDS):
            line = jnp.where(lane8 == h, STEP * coupling[f, h], line)
        line = jnp.broadcast_to(line[0:1], (R, ROWS))
        rows = jnp.where(near == 0, line, 0.0)
        rows = rows + jnp.where(owner == f, D_SCALE * diffusivity[f] * second, 0.0)
        high, rest = split(rows)
        spot = pl.ds(f * R, R)
        la[spot, 0:HALF] = high[:, 0:HALF]
        la[spot, HALF : 2 * HALF] = high[:, 0:HALF]
        la[spot, 2 * HALF : 3 * HALF] = high[:, HALF:]
        la[spot, 3 * HALF :] = high[:, HALF:]
        mlo[spot, :] = rest
    row = lax.broadcasted_iota(jnp.int32, (HALF, HALF), 0)
    col = lax.broadcasted_iota(jnp.int32, (HALF, HALF), 1)
    step = jnp.where((row >> 6) == (col >> 6), col - row, 9)
    first = jnp.where(step == 1, 8.0, jnp.where(step == -1, -8.0, 0.0))
    first = first - jnp.where(step == 2, 1.0, 0.0) + jnp.where(step == -2, 1.0, 0.0)
    band[:, 0:HALF] = first.astype(BF16)
    band[:, HALF:] = first.astype(BF16)


def prepare_kernel(
    coupling, diffusivity, state, across, inside, hilo, borders, first_cols, last_cols, la, mlo, band,
    planes, sems, send_sems,
):
    order = (0, 1, 6, 7, 2, 3, 4, 5)
    even = lax.rem(lax.axis_index("colat"), 2) == 0

    def sends(low_to, high_to):
        return [
            pltpu.make_async_copy(planes.at[0:2], low_to, send_sems.at[0]),
            pltpu.make_async_copy(planes.at[6:8], high_to, send_sems.at[1]),
        ]

    reads = {t: pltpu.make_async_copy(state.at[:, t, :], planes.at[t], sems.at[t]) for t in order}
    for t in order:
        reads[t].start()
    build_matrices(coupling, diffusivity, la, mlo, band)
    for t in EDGE_PLANES:
        reads[t].wait()

    @pl.when(even)
    def _():
        for copy in sends(across, inside):
            copy.start()

    @pl.when(jnp.logical_not(even))
    def _():
        for copy in sends(inside, across):
            copy.start()

    lane = lax.broadcasted_iota(jnp.int32, (R, LANES), 1)
    for t in order:
        if t not in EDGE_PLANES:
            reads[t].wait()

        def field(f, carry, t=t):
            block = planes[t, pl.ds(pl.multiple_of(f * R, R), R), :]
            high, rest = split(block)
            row = pl.multiple_of(f * R + (f >> 2) * HALF, R)
            cols = slice((t % 2) * LT, (t % 2 + 1) * LT)
            hilo[t // 2, pl.ds(row, R), cols] = high
            hilo[t // 2, pl.ds(row + HALF, R), cols] = rest
            tile0, tile1, tile2 = (block[:, k * LANES : (k + 1) * LANES] for k in range(3))
            seam0 = pltpu.roll(jnp.where(lane >= 64, tile0, tile1), SEAM + 2, 1)
            seam1 = pltpu.roll(jnp.where(lane >= 64, tile1, tile2), SEAM + 6, 1)
            seam = jnp.where(lane < SEAM + 4, seam0, seam1)
            seam = jnp.where((lane >= SEAM) & (lane < SEAM + 8), seam, 0.0)
            high, rest = split(seam)
            borders[t, pl.ds(row, R), :] = high
            borders[t, pl.ds(row + HALF, R), :] = rest
            spot = f * 2 * CT + 2 * t
            ends = pltpu.roll(jnp.where(lane < 64, tile0, tile2), spot, 1)
            first_cols[...] = jnp.where((lane >= spot) & (lane < spot + 2), ends, first_cols[...])
            before = (spot + LANES - 2) & (LANES - 1)
            last_cols[...] = jnp.where((lane >= before) & (lane < before + 2), ends, last_cols[...])
            return carry

        lax.fori_loop(0, FIELDS, field, 0, unroll=4)
    for copy in sends(across, inside):
        copy.wait()


def build_weights(asked, start, width, whi, wlo):
    block = min(width, 256)
    for at in range(0, width, block):
        lanes = slice(start + at, start + at + block)
        q = asked[0:1, lanes]
        a = asked[1:2, lanes]
        b = asked[2:3, lanes]
        row = ((q + 0.5) * (1.0 / LT)).astype(jnp.int32)
        col = jnp.broadcast_to(q.astype(jnp.int32) - LT * row, (16, block))
        b = jnp.broadcast_to(b, (16, block))
        rest = 1.0 - b
        spots = [
            jnp.where(row == t, 1.0 - a, jnp.where(row == t - 1, a, 0.0)) for t in range(CT)
        ]

        def chunk(i, carry):
            cell = i * 16 + lax.broadcasted_iota(jnp.int32, (16, block), 0)
            along = jnp.where(cell == col, rest, jnp.where(cell == col + 1, b, 0.0))
            for t in range(CT):
                high, low = split(along * spots[t])
                at_row = pl.multiple_of((t % 2) * LT + i * 16, 16)
                whi[t // 2, pl.ds(at_row, 16), at : at + block] = high
                wlo[t // 2, pl.ds(at_row, 16), at : at + block] = low
            return carry

        lax.fori_loop(0, LT // 16, chunk, 0)


def dot(a, b):
    return jnp.dot(a, b, preferred_element_type=F32)


def interpolate(hilo, half, whi, wlo):
    total = None
    for p in range(PAIRS):
        both = dot(hilo[p, half * ROWS : (half + 1) * ROWS, :], whi[p])
        part = both[0:HALF] + both[HALF:] + dot(hilo[p, half * ROWS : half * ROWS + HALF, :], wlo[p])
        total = part if total is None else total + part
    return total


def column_kernel(hilo, asked, first_cols, last_cols, onward, backward, whi, wlo):
    first_grid = lax.axis_index("grid") == 0
    l = lax.axis_index("lon")
    low = l == 0
    high = l == lax.axis_size("lon") - 1
    onward[...] = jnp.where(first_grid, last_cols[...], first_cols[...])
    backward[...] = jnp.where(first_grid, first_cols[...], last_cols[...])

    @pl.when(low | high)
    def _():
        build_weights(asked, STRIP, LANES, whi, wlo)
        lane = lax.broadcasted_iota(jnp.int32, (R, LANES), 1)
        packed = jnp.zeros((R, LANES), F32)
        for half in range(2):
            got = interpolate(hilo, half, whi, wlo)
            for k in range(4):
                f = half * 4 + k
                mine = (lane >> 4) == f
                packed = jnp.where(mine, pltpu.roll(got[k * R : (k + 1) * R], f * 2 * CT, 1), packed)
        ends_ring = (first_grid & high) | (jnp.logical_not(first_grid) & low)

        @pl.when(ends_ring)
        def _():
            onward[...] = packed

        @pl.when(jnp.logical_not(ends_ring))
        def _():
            backward[...] = packed


def row_kernel(hilo, asked, across, out, whi, wlo):
    c = lax.axis_index("colat")
    edge = (c == 0) | (c == lax.axis_size("colat") - 1)

    @pl.when(jnp.logical_not(edge))
    def _():
        out[...] = across[...]

    @pl.when(edge)
    def _():
        build_weights(asked, 0, STRIP, whi, wlo)
        for half in range(2):
            got = interpolate(hilo, half, whi, wlo)
            rows = slice(half * HALF, (half + 1) * HALF)
            out[0, rows, :] = got[:, 0:LT]
            out[1, rows, :] = got[:, LT:]


def main_kernel(
    diffusivity, metric, state, section, hilo, borders, la, mlo, band, fixed, halo_rows, came_onward, came_backward,
    new_state, new_section, part,
    planes, register, lin, grad, slope, halo, bands, out_state, out_section, sems, reg_sems, out_sems,
):
    c = lax.axis_index("colat")
    l = lax.axis_index("lon")
    order = (1, 2, 0, 3)
    regs = [pltpu.make_async_copy(section.at[:, t, :], register.at[t], reg_sems.at[t]) for t in range(CT)]
    reads = [pltpu.make_async_copy(state.at[:, t, :], planes.at[t], sems.at[t]) for t in range(CT)]
    for copy in reads[0:6]:
        copy.start()
    for p in order:
        regs[2 * p].start()
        regs[2 * p + 1].start()
        if p == 1:
            reads[6].start()
            reads[7].start()
    bands[:, 0 : 2 * LANES, :] = fixed[...]
    bands[:, 2 * LANES :, :] = fixed[...]
    first_grid = lax.axis_index("grid") == 0
    left = jnp.where(first_grid, came_onward[...], came_backward[...])
    right = jnp.where(first_grid, came_backward[...], came_onward[...])
    left = jnp.where(l == 0, left, pltpu.roll(left, 2, 1))
    lane = lax.broadcasted_iota(jnp.int32, (R, LANES), 1)
    for f in range(FIELDS):
        turn = f * 2 * CT
        tile = jnp.where(
            lane < 2 * CT, pltpu.roll(left, (-turn) % LANES, 1), pltpu.roll(right, (2 * CT - turn) % LANES, 1)
        )
        high, rest = split(jnp.where(lane < SEAM, tile, 0.0))
        row = (f // 4) * ROWS + (f % 4) * R
        halo[row : row + R, :] = high
        halo[row + HALF : row + HALF + R, :] = rest
    pending = {}
    scales = [diffusivity[f] * D_SCALE for f in range(FIELDS)]
    for p in order:
        lin[...] = (
            dot(la[...], hilo[p])
            + dot(mlo[:, 0:HALF], hilo[p, 0:HALF, :])
            + dot(mlo[:, HALF:], hilo[p, ROWS : ROWS + HALF, :])
        )
        for half in range(2):
            base = half * ROWS
            grad[half * HALF : (half + 1) * HALF, :] = dot(band[...], hilo[p, base : base + ROWS, :])
        for t in (2 * p, 2 * p + 1):
            for k, side in ((0, 0), (2, 1)):
                for again in range(2):
                    at_row = again * 2 * LANES + LANES
                    bands[k, at_row : at_row + 32, :] = halo_rows[side, t]
            for half in range(2):
                base = half * ROWS
                high = slice(base, base + HALF)
                rest = slice(base + HALF, base + ROWS)
                edge_high = borders[t, high, :] + halo[high, :]
                edge_rest = borders[t, rest, :] + halo[rest, :]
                for k in range(3):
                    cols = slice((t % 2) * LT + k * LANES, (t % 2) * LT + (k + 1) * LANES)
                    wide = jnp.concatenate(
                        [hilo[p, high, cols], edge_high, hilo[p, rest, cols], edge_rest], axis=1
                    )
                    slope[t % 2, half * HALF : (half + 1) * HALF, 2 * k * LANES : 2 * (k + 1) * LANES] = dot(
                        wide, bands[k]
                    )
        both = (2 * p, 2 * p + 1)
        final = p in (1, 2)
        if p == order[0]:
            wait_all(reads[0:6])
        elif p == order[1]:
            wait_all(reads[6:])
        for t in both:
            regs[t].wait()
            if final and t % 2 in pending:
                wait_all(pending.pop(t % 2))
        inv_sin = [metric[c * CT + t] for t in both]
        inv_sin2 = [value * value for value in inv_sin]

        def block(i, carry, both=both, final=final, inv_sin=inv_sin, inv_sin2=inv_sin2):
            r0 = pl.multiple_of(i * 8, 8)
            for k in range(3):
                cols = slice(k * LANES, (k + 1) * LANES)
                d1 = slice(2 * k * LANES, (2 * k + 1) * LANES)
                d2 = slice((2 * k + 1) * LANES, (2 * k + 2) * LANES)
                vels = [[planes[t, pl.ds(v * R + r0, 8), cols] * V_SCALE for v in range(3)] for t in both]
                for n in range(2):
                    vels[n][2] = vels[n][2] * inv_sin[n]
                for f in range(FIELDS):
                    rows = pl.ds(f * R + r0, 8)
                    near_by = {t: planes[t, rows, cols] for t in range(both[0] - 2, both[1] + 3) if 0 <= t < CT}
                    for n, t in enumerate(both):
                        wide = slice(n * LT + k * LANES, n * LT + (k + 1) * LANES)
                        up1, dn1, up2, dn2 = (near_by.get(t + step) for step in (1, -1, 2, -2))
                        if up1 is None:
                            near, near_d = dn1, -dn1
                        elif dn1 is None:
                            near, near_d = up1, up1
                        else:
                            near, near_d = up1 + dn1, up1 - dn1
                        if up2 is None:
                            far, far_d = dn2, -dn2
                        elif dn2 is None:
                            far, far_d = up2, up2
                        else:
                            far, far_d = up2 + dn2, up2 - dn2
                        lap = (16.0 * near - far) + inv_sin2[n] * slope[n, rows, d2]
                        adv = (
                            vels[n][0] * grad[rows, wide]
                            + vels[n][1] * (8.0 * near_d - far_d)
                            + vels[n][2] * slope[n, rows, d1]
                        )
                        fresh = (KEEP * register[t, rows, cols] + lin[rows, wide]) + (scales[f] * lap - adv)
                        if final:
                            out_section[n, rows, cols] = fresh
                            out_state[n, rows, cols] = near_by[t] + GAIN * fresh
                        else:
                            part[EDGE_PLANES.index(t), rows, cols] = fresh
            return carry

        lax.fori_loop(0, R // 8, block, 0)
        if final:
            for t in both:
                slot = t % 2
                pending[slot] = [
                    pltpu.make_async_copy(out_section.at[slot], new_section.at[:, t, :], out_sems.at[slot, 0]),
                    pltpu.make_async_copy(out_state.at[slot], new_state.at[:, t, :], out_sems.at[slot, 1]),
                ]
                for copy in pending[slot]:
                    copy.start()
    for writes in pending.values():
        wait_all(writes)


def finish_kernel(
    diffusivity, part, across, inside, from_across, from_inside, old_state, old_section,
    new_state, new_section, out_state, out_section, out_sems,
):
    del old_state, old_section
    c = lax.axis_index("colat")
    even = lax.rem(c, 2) == 0

    def run(low, high, below, above):
        for i in range(4):
            source, received = (low, below) if i < 2 else (high, above)
            j = i % 2
            side = i // 2

            def block(n, carry, i=i, source=source, received=received, j=j, side=side):
                f = n // 4
                rows = pl.ds(pl.multiple_of(n * 16, 16), 16)
                r0 = pl.multiple_of(R + lax.rem(n, 4) * 16, 16)
                diffuse = diffusivity[f] * D_SCALE
                vel = source[j, pl.ds(r0, 16), :] * V_SCALE
                near = received[1 - side, rows, :]
                if i in (0, 3):
                    outer = received[side, rows, :]
                    vel = vel if i == 0 else -vel
                    fix = diffuse * (16.0 * near - outer) + vel * (8.0 * near - outer)
                else:
                    fix = -(diffuse + vel) * near if i == 1 else -(diffuse - vel) * near
                fresh = part[i, rows, :] + fix
                out_section[i, rows, :] = fresh
                out_state[i, rows, :] = source[j, rows, :] + GAIN * fresh
                return carry

            lax.fori_loop(0, ROWS // 16, block, 0, unroll=2)
            for copy in writes(i):
                copy.start()

    def writes(i):
        t = EDGE_PLANES[i]
        return [
            pltpu.make_async_copy(out_section.at[i], new_section.at[:, t, :], out_sems.at[i, 0]),
            pltpu.make_async_copy(out_state.at[i], new_state.at[:, t, :], out_sems.at[i, 1]),
        ]

    @pl.when(even)
    def _():
        run(across, inside, from_across, from_inside)

    @pl.when(jnp.logical_not(even))
    def _():
        run(inside, across, from_inside, from_across)

    for i in range(4):
        wait_all(writes(i))


def sds(shape, kind=F32):
    return jax.ShapeDtypeStruct(shape, kind)


def params(mib):
    return pltpu.CompilerParams(vmem_limit_bytes=mib * 2**20)


def cost(us):
    return pl.CostEstimate(flops=us * 10**9, bytes_accessed=us * 3 * 10**6, transcendentals=0)


def at(g, c, l, sizes):
    return (g * sizes[1] + c) * sizes[2] + l


def local(state, section, diffusivity, coupling, pairs, fractions):
    sizes = tuple(lax.axis_size(axis) for axis in AXES)
    grids, tiles_c, tiles_l = sizes
    tiles = [(g, c, l) for g in range(grids) for c in range(tiles_c) for l in range(tiles_l)]

    def mates(chosen):
        return [(at(g, c, l, sizes), at(1 - g, c, l, sizes)) for g, c, l in tiles if chosen(c, l)]

    def on_rows(c, l):
        return c in (0, tiles_c - 1)

    def on_cols(c, l):
        return l in (0, tiles_l - 1)

    fields = state.reshape(ROWS, CT, LT)
    register = section.reshape(ROWS, CT, LT)
    request = jnp.concatenate([pairs.reshape(1, -1).astype(F32), fractions.reshape(2, -1)], axis=0)
    request = jnp.pad(request, ((0, 0), (0, STRIP + LANES - request.shape[1])))
    plane2 = sds((2, ROWS, LT))
    halo2 = sds((R, LANES))
    request, fields = lax.optimization_barrier((request, fields))
    asked = lax.ppermute(request, AXES, mates(lambda c, l: on_rows(c, l) or on_cols(c, l)))
    across, inside, hilo, borders, first_cols, last_cols, la, mlo, band = pl.pallas_call(
        prepare_kernel,
        out_shape=(
            plane2, plane2, sds((PAIRS, 2 * ROWS, 2 * LT), BF16), sds((CT, 2 * ROWS, LANES), BF16), halo2, halo2,
            sds((ROWS, 2 * ROWS), BF16), sds((ROWS, ROWS), BF16), sds((HALF, ROWS), BF16),
        ),
        in_specs=[SM, SM, ANY],
        out_specs=(ANY, ANY) + (VM,) * 7,
        scratch_shapes=[
            pltpu.VMEM((CT, ROWS, LT), F32), pltpu.SemaphoreType.DMA((CT,)), pltpu.SemaphoreType.DMA((2,)),
        ],
        compiler_params=params(38),
        cost_estimate=cost(8),
        name="prepare",
    )(coupling, diffusivity, fields)
    first_cols, last_cols, asked = lax.optimization_barrier((first_cols, last_cols, asked))
    onward, backward = pl.pallas_call(
        column_kernel,
        out_shape=(halo2, halo2),
        in_specs=[VM] * 4,
        out_specs=(VM, VM),
        scratch_shapes=[pltpu.VMEM((PAIRS, 2 * LT, LANES), BF16)] * 2,
        compiler_params=params(16),
        name="border_columns",
    )(hilo, asked, first_cols, last_cols)
    ring = []
    for g, c, l in tiles:
        ends = (g == 0 and l == tiles_l - 1) or (g == 1 and l == 0)
        to = (1 - g, c, l) if ends else (g, c, l + 1 - 2 * g)
        ring.append((at(g, c, l, sizes), at(*to, sizes)))
    came_onward = lax.ppermute(onward, AXES, ring)
    came_backward = lax.ppermute(backward, AXES, [(j, i) for i, j in ring])
    step_inside = [(i, i + 1) for i in range(0, tiles_c, 2)]
    inside, onward, backward = lax.optimization_barrier((inside, onward, backward))
    from_inside = lax.ppermute(inside, "colat", step_inside + [(j, i) for i, j in step_inside])
    hilo, onward = lax.optimization_barrier((hilo, onward))
    served = pl.pallas_call(
        row_kernel,
        out_shape=plane2,
        in_specs=[VM, VM, VM],
        out_specs=VM,
        scratch_shapes=[pltpu.VMEM((PAIRS, 2 * LT, STRIP), BF16)] * 2,
        compiler_params=params(24),
        cost_estimate=cost(5),
        name="border_rows",
    )(hilo, asked, across)
    served, came_onward, came_backward = lax.optimization_barrier((served, came_onward, came_backward))
    exchange = mates(on_rows)
    for g, c, l in tiles:
        if not on_rows(c, l):
            exchange.append((at(g, c, l, sizes), at(g, c + 1 if c % 2 else c - 1, l, sizes)))
    from_across = lax.ppermute(served, AXES, exchange)

    theta = math.pi / 4 + (np.arange(tiles_c * CT) + 0.5) * (math.pi / 2) / (tiles_c * CT)
    metric = jnp.asarray((1.0 / np.sin(theta)).astype(np.float32))
    whole = sds((ROWS, CT, LT))
    fixed, halo_rows = (jnp.asarray(value, BF16) for value in longitude_bands())
    new_state, new_section, part = pl.pallas_call(
        main_kernel,
        out_shape=(whole, whole, sds((4, ROWS, LT))),
        in_specs=[SM, SM, ANY, ANY] + [VM] * 9,
        out_specs=(ANY, ANY, VM),
        scratch_shapes=[
            pltpu.VMEM((CT, ROWS, LT), F32),
            pltpu.VMEM((CT, ROWS, LT), F32),
            pltpu.VMEM((ROWS, 2 * LT), F32),
            pltpu.VMEM((ROWS, 2 * LT), F32),
            pltpu.VMEM((2, ROWS, 2 * LT), F32),
            pltpu.VMEM((2 * ROWS, LANES), BF16),
            pltpu.VMEM((3, 4 * LANES, 2 * LANES), BF16),
            pltpu.VMEM((2, ROWS, LT), F32),
            pltpu.VMEM((2, ROWS, LT), F32),
            pltpu.SemaphoreType.DMA((CT,)),
            pltpu.SemaphoreType.DMA((CT,)),
            pltpu.SemaphoreType.DMA((2, 2)),
        ],
        compiler_params=params(38),
        name="interior",
    )(
        diffusivity, metric, fields, register, hilo, borders, la, mlo, band, fixed, halo_rows,
        came_onward, came_backward,
    )

    new_state, new_section = pl.pallas_call(
        finish_kernel,
        out_shape=(whole, whole),
        in_specs=[SM, VM, VM, VM, VM, VM, ANY, ANY],
        out_specs=(ANY, ANY),
        scratch_shapes=[
            pltpu.VMEM((4, ROWS, LT), F32),
            pltpu.VMEM((4, ROWS, LT), F32),
            pltpu.SemaphoreType.DMA((4, 2)),
        ],
        input_output_aliases={6: 0, 7: 1},
        compiler_params=params(12),
        name="finish_edges",
    )(diffusivity, part, across, inside, from_across, from_inside, new_state, new_section)
    return new_state.reshape(state.shape), new_section.reshape(section.shape)


def solution(mesh):
    field = P("grid", None, None, "colat", "lon")
    placed = (field, field, P(), P(), P("grid", "colat", "lon", None), P("grid", "colat", "lon", None, None))
    return jax.shard_map(
        local, mesh=mesh, in_specs=placed, out_specs=(field, field), check_vma=False
    )
```

```python
import functools
import math

import jax
import jax.numpy as jnp
import numpy as np
from jax import lax
from jax.experimental import pallas as pl
from jax.experimental.pallas import tpu as pltpu
from jax.sharding import PartitionSpec as P

FIELDS = 8
R = 64
CT = 8
LT = 384
ROWS = FIELDS * R
HALF = ROWS // 2
PAIRS = CT // 2
STRIP = 2 * LT
LANES = 128
AXES = ("grid", "colat", "lon")

KEEP = -5.0 / 9.0
GAIN = 15.0 / 16.0
STEP = 0.25
D_SCALE = STEP / 12.0
V_SCALE = STEP * 0.5 / 12.0

F32 = jnp.float32
BF16 = jnp.bfloat16
ANY = pl.BlockSpec(memory_space=pl.ANY)
VM = pl.BlockSpec(memory_space=pltpu.VMEM)
SM = pl.BlockSpec(memory_space=pltpu.SMEM)
EDGE_PLANES = (0, 1, 6, 7)
SEAM = 32
FIRST = {1: 8.0, -1: -8.0, 2: -1.0, -2: 1.0}
SECOND = {0: -30.0, 1: 16.0, -1: 16.0, 2: -1.0, -2: -1.0}


def longitude_bands():
    fixed = np.zeros((3, 2 * LANES, 2 * LANES), np.float32)
    halo = np.zeros((2, CT, 32, 2 * LANES), np.float32)
    for k in range(3):
        for n in range(LANES):
            for base, stencil in ((0, FIRST), (LANES, SECOND)):
                for offset, value in stencil.items():
                    y = k * LANES + n + offset
                    if y < 0:
                        for t in range(CT):
                            halo[0, t, 2 * t + y + 2, base + n] = value
                    elif y >= LT:
                        for t in range(CT):
                            halo[1, t, 2 * CT + 2 * t + y - LT, base + n] = value
                    elif y // LANES == k:
                        fixed[k, y - k * LANES, base + n] = value
                    else:
                        lane = SEAM + y - 126 if y < LANES + 2 else SEAM + 4 + y - 254
                        fixed[k, LANES + lane, base + n] = value
    return fixed, halo


def split(value):
    high = value.astype(BF16)
    return high, (value - high.astype(F32)).astype(BF16)


def wait_all(copies):
    for copy in copies:
        copy.wait()


def build_matrices(coupling, diffusivity, la, mlo, band):
    lane = lax.broadcasted_iota(jnp.int32, (R, ROWS), 1)
    away = (lane & (R - 1)) - lax.broadcasted_iota(jnp.int32, (R, ROWS), 0)
    owner = lane >> 6
    near = jnp.abs(away)
    second = jnp.where(near == 0, -60.0, jnp.where(near == 1, 16.0, jnp.where(near == 2, -1.0, 0.0)))
    lane8 = lax.broadcasted_iota(jnp.int32, (8, ROWS), 1) >> 6
    for f in range(FIELDS):
        line = jnp.zeros((8, ROWS), F32)
        for h in range(FIELDS):
            line = jnp.where(lane8 == h, STEP * coupling[f, h], line)
        line = jnp.broadcast_to(line[0:1], (R, ROWS))
        rows = jnp.where(near == 0, line, 0.0)
        rows = rows + jnp.where(owner == f, D_SCALE * diffusivity[f] * second, 0.0)
        high, rest = split(rows)
        spot = pl.ds(f * R, R)
        la[spot, 0:HALF] = high[:, 0:HALF]
        la[spot, HALF : 2 * HALF] = high[:, 0:HALF]
        la[spot, 2 * HALF : 3 * HALF] = high[:, HALF:]
        la[spot, 3 * HALF :] = high[:, HALF:]
        mlo[spot, :] = rest
    row = lax.broadcasted_iota(jnp.int32, (HALF, HALF), 0)
    col = lax.broadcasted_iota(jnp.int32, (HALF, HALF), 1)
    step = jnp.where((row >> 6) == (col >> 6), col - row, 9)
    first = jnp.where(step == 1, 8.0, jnp.where(step == -1, -8.0, 0.0))
    first = first - jnp.where(step == 2, 1.0, 0.0) + jnp.where(step == -2, 1.0, 0.0)
    band[:, 0:HALF] = first.astype(BF16)
    band[:, HALF:] = first.astype(BF16)


def prepare_kernel(
    coupling, diffusivity, state, across, inside, hilo, borders, first_cols, last_cols, la, mlo, band,
    planes, sems, send_sems,
):
    order = (0, 1, 6, 7, 2, 3, 4, 5)
    even = lax.rem(lax.axis_index("colat"), 2) == 0

    def sends(low_to, high_to):
        return [
            pltpu.make_async_copy(planes.at[0:2], low_to, send_sems.at[0]),
            pltpu.make_async_copy(planes.at[6:8], high_to, send_sems.at[1]),
        ]

    reads = {t: pltpu.make_async_copy(state.at[:, t, :], planes.at[t], sems.at[t]) for t in order}
    for t in order:
        reads[t].start()
    build_matrices(coupling, diffusivity, la, mlo, band)
    for t in EDGE_PLANES:
        reads[t].wait()

    @pl.when(even)
    def _():
        for copy in sends(across, inside):
            copy.start()

    @pl.when(jnp.logical_not(even))
    def _():
        for copy in sends(inside, across):
            copy.start()

    lane = lax.broadcasted_iota(jnp.int32, (R, LANES), 1)
    for t in order:
        if t not in EDGE_PLANES:
            reads[t].wait()

        def field(f, carry, t=t):
            block = planes[t, pl.ds(pl.multiple_of(f * R, R), R), :]
            high, rest = split(block)
            row = pl.multiple_of(f * R + (f >> 2) * HALF, R)
            cols = slice((t % 2) * LT, (t % 2 + 1) * LT)
            hilo[t // 2, pl.ds(row, R), cols] = high
            hilo[t // 2, pl.ds(row + HALF, R), cols] = rest
            tile0, tile1, tile2 = (block[:, k * LANES : (k + 1) * LANES] for k in range(3))
            seam0 = pltpu.roll(jnp.where(lane >= 64, tile0, tile1), SEAM + 2, 1)
            seam1 = pltpu.roll(jnp.where(lane >= 64, tile1, tile2), SEAM + 6, 1)
            seam = jnp.where(lane < SEAM + 4, seam0, seam1)
            seam = jnp.where((lane >= SEAM) & (lane < SEAM + 8), seam, 0.0)
            high, rest = split(seam)
            borders[t, pl.ds(row, R), :] = high
            borders[t, pl.ds(row + HALF, R), :] = rest
            spot = f * 2 * CT + 2 * t
            ends = pltpu.roll(jnp.where(lane < 64, tile0, tile2), spot, 1)
            first_cols[...] = jnp.where((lane >= spot) & (lane < spot + 2), ends, first_cols[...])
            before = (spot + LANES - 2) & (LANES - 1)
            last_cols[...] = jnp.where((lane >= before) & (lane < before + 2), ends, last_cols[...])
            return carry

        lax.fori_loop(0, FIELDS, field, 0, unroll=4)
    for copy in sends(across, inside):
        copy.wait()


def build_weights(asked, start, width, whi, wlo):
    block = min(width, 256)
    for at in range(0, width, block):
        lanes = slice(start + at, start + at + block)
        q = asked[0:1, lanes]
        a = asked[1:2, lanes]
        b = asked[2:3, lanes]
        row = ((q + 0.5) * (1.0 / LT)).astype(jnp.int32)
        col = jnp.broadcast_to(q.astype(jnp.int32) - LT * row, (16, block))
        b = jnp.broadcast_to(b, (16, block))
        rest = 1.0 - b
        spots = [
            jnp.where(row == t, 1.0 - a, jnp.where(row == t - 1, a, 0.0)) for t in range(CT)
        ]

        def chunk(i, carry):
            cell = i * 16 + lax.broadcasted_iota(jnp.int32, (16, block), 0)
            along = jnp.where(cell == col, rest, jnp.where(cell == col + 1, b, 0.0))
            for t in range(CT):
                high, low = split(along * spots[t])
                at_row = pl.multiple_of((t % 2) * LT + i * 16, 16)
                whi[t // 2, pl.ds(at_row, 16), at : at + block] = high
                wlo[t // 2, pl.ds(at_row, 16), at : at + block] = low
            return carry

        lax.fori_loop(0, LT // 16, chunk, 0)


def dot(a, b):
    return jnp.dot(a, b, preferred_element_type=F32)


def interpolate(hilo, half, whi, wlo):
    total = None
    for p in range(PAIRS):
        both = dot(hilo[p, half * ROWS : (half + 1) * ROWS, :], whi[p])
        part = both[0:HALF] + both[HALF:] + dot(hilo[p, half * ROWS : half * ROWS + HALF, :], wlo[p])
        total = part if total is None else total + part
    return total


def column_kernel(hilo, asked, first_cols, last_cols, onward, backward, whi, wlo):
    first_grid = lax.axis_index("grid") == 0
    l = lax.axis_index("lon")
    low = l == 0
    high = l == lax.axis_size("lon") - 1
    onward[...] = jnp.where(first_grid, last_cols[...], first_cols[...])
    backward[...] = jnp.where(first_grid, first_cols[...], last_cols[...])

    @pl.when(low | high)
    def _():
        build_weights(asked, STRIP, LANES, whi, wlo)
        lane = lax.broadcasted_iota(jnp.int32, (R, LANES), 1)
        packed = jnp.zeros((R, LANES), F32)
        for half in range(2):
            got = interpolate(hilo, half, whi, wlo)
            for k in range(4):
                f = half * 4 + k
                mine = (lane >> 4) == f
                packed = jnp.where(mine, pltpu.roll(got[k * R : (k + 1) * R], f * 2 * CT, 1), packed)
        ends_ring = (first_grid & high) | (jnp.logical_not(first_grid) & low)

        @pl.when(ends_ring)
        def _():
            onward[...] = packed

        @pl.when(jnp.logical_not(ends_ring))
        def _():
            backward[...] = packed


def row_kernel(hilo, asked, across, out, whi, wlo):
    c = lax.axis_index("colat")
    edge = (c == 0) | (c == lax.axis_size("colat") - 1)

    @pl.when(jnp.logical_not(edge))
    def _():
        out[...] = across[...]

    @pl.when(edge)
    def _():
        build_weights(asked, 0, STRIP, whi, wlo)
        for half in range(2):
            got = interpolate(hilo, half, whi, wlo)
            rows = slice(half * HALF, (half + 1) * HALF)
            out[0, rows, :] = got[:, 0:LT]
            out[1, rows, :] = got[:, LT:]


def main_kernel(
    diffusivity, metric, state, section, split_state, borders, la, mlo, band, fixed, halo_rows, came_onward, came_backward,
    new_state, new_section, part,
    hilo, planes, register, lin, grad, slope, halo, bands, out_state, out_section,
    split_sems, sems, reg_sems, out_sems,
):
    c = lax.axis_index("colat")
    l = lax.axis_index("lon")
    order = (1, 2, 0, 3)
    regs = [pltpu.make_async_copy(section.at[:, t, :], register.at[t], reg_sems.at[t]) for t in range(CT)]
    reads = [pltpu.make_async_copy(state.at[:, t, :], planes.at[t], sems.at[t]) for t in range(CT)]
    splits = [pltpu.make_async_copy(split_state.at[p], hilo.at[p], split_sems.at[p]) for p in range(PAIRS)]
    splits[order[0]].start()
    for copy in reads[0:6]:
        copy.start()
    for p in order:
        if p != order[0]:
            splits[p].start()
        regs[2 * p].start()
        regs[2 * p + 1].start()
        if p == 1:
            reads[6].start()
            reads[7].start()
    bands[:, 0 : 2 * LANES, :] = fixed[...]
    bands[:, 2 * LANES :, :] = fixed[...]
    first_grid = lax.axis_index("grid") == 0
    left = jnp.where(first_grid, came_onward[...], came_backward[...])
    right = jnp.where(first_grid, came_backward[...], came_onward[...])
    left = jnp.where(l == 0, left, pltpu.roll(left, 2, 1))
    lane = lax.broadcasted_iota(jnp.int32, (R, LANES), 1)
    for f in range(FIELDS):
        turn = f * 2 * CT
        tile = jnp.where(
            lane < 2 * CT, pltpu.roll(left, (-turn) % LANES, 1), pltpu.roll(right, (2 * CT - turn) % LANES, 1)
        )
        high, rest = split(jnp.where(lane < SEAM, tile, 0.0))
        row = (f // 4) * ROWS + (f % 4) * R
        halo[row : row + R, :] = high
        halo[row + HALF : row + HALF + R, :] = rest
    pending = {}
    scales = [diffusivity[f] * D_SCALE for f in range(FIELDS)]
    for p in order:
        splits[p].wait()
        lin[...] = (
            dot(la[...], hilo[p])
            + dot(mlo[:, 0:HALF], hilo[p, 0:HALF, :])
            + dot(mlo[:, HALF:], hilo[p, ROWS : ROWS + HALF, :])
        )
        for half in range(2):
            base = half * ROWS
            grad[half * HALF : (half + 1) * HALF, :] = dot(band[...], hilo[p, base : base + ROWS, :])
        for t in (2 * p, 2 * p + 1):
            for k, side in ((0, 0), (2, 1)):
                for again in range(2):
                    at_row = again * 2 * LANES + LANES
                    bands[k, at_row : at_row + 32, :] = halo_rows[side, t]
            for half in range(2):
                base = half * ROWS
                high = slice(base, base + HALF)
                rest = slice(base + HALF, base + ROWS)
                edge_high = borders[t, high, :] + halo[high, :]
                edge_rest = borders[t, rest, :] + halo[rest, :]
                for k in range(3):
                    cols = slice((t % 2) * LT + k * LANES, (t % 2) * LT + (k + 1) * LANES)
                    wide = jnp.concatenate(
                        [hilo[p, high, cols], edge_high, hilo[p, rest, cols], edge_rest], axis=1
                    )
                    slope[t % 2, half * HALF : (half + 1) * HALF, 2 * k * LANES : 2 * (k + 1) * LANES] = dot(
                        wide, bands[k]
                    )
        both = (2 * p, 2 * p + 1)
        final = p in (1, 2)
        if p == order[0]:
            wait_all(reads[0:6])
        elif p == order[1]:
            wait_all(reads[6:])
        for t in both:
            regs[t].wait()
            if final and t % 2 in pending:
                wait_all(pending.pop(t % 2))
        inv_sin = [metric[c * CT + t] for t in both]
        inv_sin2 = [value * value for value in inv_sin]

        def block(i, carry, both=both, final=final, inv_sin=inv_sin, inv_sin2=inv_sin2):
            r0 = pl.multiple_of(i * 8, 8)
            for k in range(3):
                cols = slice(k * LANES, (k + 1) * LANES)
                d1 = slice(2 * k * LANES, (2 * k + 1) * LANES)
                d2 = slice((2 * k + 1) * LANES, (2 * k + 2) * LANES)
                vels = [[planes[t, pl.ds(v * R + r0, 8), cols] * V_SCALE for v in range(3)] for t in both]
                for n in range(2):
                    vels[n][2] = vels[n][2] * inv_sin[n]
                for f in range(FIELDS):
                    rows = pl.ds(f * R + r0, 8)
                    near_by = {t: planes[t, rows, cols] for t in range(both[0] - 2, both[1] + 3) if 0 <= t < CT}
                    for n, t in enumerate(both):
                        wide = slice(n * LT + k * LANES, n * LT + (k + 1) * LANES)
                        up1, dn1, up2, dn2 = (near_by.get(t + step) for step in (1, -1, 2, -2))
                        if up1 is None:
                            near, near_d = dn1, -dn1
                        elif dn1 is None:
                            near, near_d = up1, up1
                        else:
                            near, near_d = up1 + dn1, up1 - dn1
                        if up2 is None:
                            far, far_d = dn2, -dn2
                        elif dn2 is None:
                            far, far_d = up2, up2
                        else:
                            far, far_d = up2 + dn2, up2 - dn2
                        lap = (16.0 * near - far) + inv_sin2[n] * slope[n, rows, d2]
                        adv = (
                            vels[n][0] * grad[rows, wide]
                            + vels[n][1] * (8.0 * near_d - far_d)
                            + vels[n][2] * slope[n, rows, d1]
                        )
                        fresh = (KEEP * register[t, rows, cols] + lin[rows, wide]) + (scales[f] * lap - adv)
                        if final:
                            out_section[n, rows, cols] = fresh
                            out_state[n, rows, cols] = near_by[t] + GAIN * fresh
                        else:
                            part[EDGE_PLANES.index(t), rows, cols] = fresh
            return carry

        lax.fori_loop(0, R // 8, block, 0)
        if final:
            for t in both:
                slot = t % 2
                pending[slot] = [
                    pltpu.make_async_copy(out_section.at[slot], new_section.at[:, t, :], out_sems.at[slot, 0]),
                    pltpu.make_async_copy(out_state.at[slot], new_state.at[:, t, :], out_sems.at[slot, 1]),
                ]
                for copy in pending[slot]:
                    copy.start()
    for writes in pending.values():
        wait_all(writes)


def finish_kernel(
    diffusivity, part, across, inside, from_across, from_inside, old_state, old_section,
    new_state, new_section, out_state, out_section, out_sems,
):
    del old_state, old_section
    c = lax.axis_index("colat")
    even = lax.rem(c, 2) == 0

    def run(low, high, below, above):
        for i in range(4):
            source, received = (low, below) if i < 2 else (high, above)
            j = i % 2
            side = i // 2

            def block(n, carry, i=i, source=source, received=received, j=j, side=side):
                f = n // 4
                rows = pl.ds(pl.multiple_of(n * 16, 16), 16)
                r0 = pl.multiple_of(R + lax.rem(n, 4) * 16, 16)
                diffuse = diffusivity[f] * D_SCALE
                vel = source[j, pl.ds(r0, 16), :] * V_SCALE
                near = received[1 - side, rows, :]
                if i in (0, 3):
                    outer = received[side, rows, :]
                    vel = vel if i == 0 else -vel
                    fix = diffuse * (16.0 * near - outer) + vel * (8.0 * near - outer)
                else:
                    fix = -(diffuse + vel) * near if i == 1 else -(diffuse - vel) * near
                fresh = part[i, rows, :] + fix
                out_section[i, rows, :] = fresh
                out_state[i, rows, :] = source[j, rows, :] + GAIN * fresh
                return carry

            lax.fori_loop(0, ROWS // 16, block, 0, unroll=2)
            for copy in writes(i):
                copy.start()

    def writes(i):
        t = EDGE_PLANES[i]
        return [
            pltpu.make_async_copy(out_section.at[i], new_section.at[:, t, :], out_sems.at[i, 0]),
            pltpu.make_async_copy(out_state.at[i], new_state.at[:, t, :], out_sems.at[i, 1]),
        ]

    @pl.when(even)
    def _():
        run(across, inside, from_across, from_inside)

    @pl.when(jnp.logical_not(even))
    def _():
        run(inside, across, from_inside, from_across)

    for i in range(4):
        wait_all(writes(i))


def sds(shape, kind=F32):
    return jax.ShapeDtypeStruct(shape, kind)


def params(mib):
    return pltpu.CompilerParams(vmem_limit_bytes=mib * 2**20)


def cost(us):
    return pl.CostEstimate(flops=us * 10**9, bytes_accessed=us * 3 * 10**6, transcendentals=0)


def at(g, c, l, sizes):
    return (g * sizes[1] + c) * sizes[2] + l


def local(state, section, diffusivity, coupling, pairs, fractions):
    sizes = tuple(lax.axis_size(axis) for axis in AXES)
    grids, tiles_c, tiles_l = sizes
    tiles = [(g, c, l) for g in range(grids) for c in range(tiles_c) for l in range(tiles_l)]

    def mates(chosen):
        return [(at(g, c, l, sizes), at(1 - g, c, l, sizes)) for g, c, l in tiles if chosen(c, l)]

    def on_rows(c, l):
        return c in (0, tiles_c - 1)

    def on_cols(c, l):
        return l in (0, tiles_l - 1)

    fields = state.reshape(ROWS, CT, LT)
    register = section.reshape(ROWS, CT, LT)
    request = jnp.concatenate([pairs.reshape(1, -1).astype(F32), fractions.reshape(2, -1)], axis=0)
    request = jnp.pad(request, ((0, 0), (0, STRIP + LANES - request.shape[1])))
    plane2 = sds((2, ROWS, LT))
    halo2 = sds((R, LANES))
    request, fields = lax.optimization_barrier((request, fields))
    asked = lax.ppermute(request, AXES, mates(lambda c, l: on_rows(c, l) or on_cols(c, l)))
    across, inside, hilo, borders, first_cols, last_cols, la, mlo, band = pl.pallas_call(
        prepare_kernel,
        out_shape=(
            plane2, plane2, sds((PAIRS, 2 * ROWS, 2 * LT), BF16), sds((CT, 2 * ROWS, LANES), BF16), halo2, halo2,
            sds((ROWS, 2 * ROWS), BF16), sds((ROWS, ROWS), BF16), sds((HALF, ROWS), BF16),
        ),
        in_specs=[SM, SM, ANY],
        out_specs=(ANY, ANY) + (VM,) * 7,
        scratch_shapes=[
            pltpu.VMEM((CT, ROWS, LT), F32), pltpu.SemaphoreType.DMA((CT,)), pltpu.SemaphoreType.DMA((2,)),
        ],
        compiler_params=params(38),
        cost_estimate=cost(8),
        name="prepare",
    )(coupling, diffusivity, fields)
    first_cols, last_cols, asked = lax.optimization_barrier((first_cols, last_cols, asked))
    onward, backward = pl.pallas_call(
        column_kernel,
        out_shape=(halo2, halo2),
        in_specs=[VM] * 4,
        out_specs=(VM, VM),
        scratch_shapes=[pltpu.VMEM((PAIRS, 2 * LT, LANES), BF16)] * 2,
        compiler_params=params(16),
        name="border_columns",
    )(hilo, asked, first_cols, last_cols)
    ring = []
    for g, c, l in tiles:
        ends = (g == 0 and l == tiles_l - 1) or (g == 1 and l == 0)
        to = (1 - g, c, l) if ends else (g, c, l + 1 - 2 * g)
        ring.append((at(g, c, l, sizes), at(*to, sizes)))
    came_onward = lax.ppermute(onward, AXES, ring)
    came_backward = lax.ppermute(backward, AXES, [(j, i) for i, j in ring])
    step_inside = [(i, i + 1) for i in range(0, tiles_c, 2)]
    inside, onward, backward = lax.optimization_barrier((inside, onward, backward))
    from_inside = lax.ppermute(inside, "colat", step_inside + [(j, i) for i, j in step_inside])
    hilo, onward = lax.optimization_barrier((hilo, onward))
    served = pl.pallas_call(
        row_kernel,
        out_shape=plane2,
        in_specs=[VM, VM, VM],
        out_specs=VM,
        scratch_shapes=[pltpu.VMEM((PAIRS, 2 * LT, STRIP), BF16)] * 2,
        compiler_params=params(24),
        cost_estimate=cost(5),
        name="border_rows",
    )(hilo, asked, across)
    served, came_onward, came_backward = lax.optimization_barrier((served, came_onward, came_backward))
    exchange = mates(on_rows)
    for g, c, l in tiles:
        if not on_rows(c, l):
            exchange.append((at(g, c, l, sizes), at(g, c + 1 if c % 2 else c - 1, l, sizes)))
    from_across = lax.ppermute(served, AXES, exchange)

    theta = math.pi / 4 + (np.arange(tiles_c * CT) + 0.5) * (math.pi / 2) / (tiles_c * CT)
    metric = jnp.asarray((1.0 / np.sin(theta)).astype(np.float32))
    whole = sds((ROWS, CT, LT))
    fixed, halo_rows = (jnp.asarray(value, BF16) for value in longitude_bands())
    new_state, new_section, part = pl.pallas_call(
        main_kernel,
        out_shape=(whole, whole, sds((4, ROWS, LT))),
        in_specs=[SM, SM, ANY, ANY, ANY] + [VM] * 8,
        out_specs=(ANY, ANY, VM),
        scratch_shapes=[
            pltpu.VMEM((PAIRS, 2 * ROWS, 2 * LT), BF16),
            pltpu.VMEM((CT, ROWS, LT), F32),
            pltpu.VMEM((CT, ROWS, LT), F32),
            pltpu.VMEM((ROWS, 2 * LT), F32),
            pltpu.VMEM((ROWS, 2 * LT), F32),
            pltpu.VMEM((2, ROWS, 2 * LT), F32),
            pltpu.VMEM((2 * ROWS, LANES), BF16),
            pltpu.VMEM((3, 4 * LANES, 2 * LANES), BF16),
            pltpu.VMEM((2, ROWS, LT), F32),
            pltpu.VMEM((2, ROWS, LT), F32),
            pltpu.SemaphoreType.DMA((PAIRS,)),
            pltpu.SemaphoreType.DMA((CT,)),
            pltpu.SemaphoreType.DMA((CT,)),
            pltpu.SemaphoreType.DMA((2, 2)),
        ],
        compiler_params=params(38),
        name="interior",
    )(
        diffusivity, metric, fields, register, hilo, borders, la, mlo, band, fixed, halo_rows,
        came_onward, came_backward,
    )

    new_state, new_section = pl.pallas_call(
        finish_kernel,
        out_shape=(whole, whole),
        in_specs=[SM, VM, VM, VM, VM, VM, ANY, ANY],
        out_specs=(ANY, ANY),
        scratch_shapes=[
            pltpu.VMEM((4, ROWS, LT), F32),
            pltpu.VMEM((4, ROWS, LT), F32),
            pltpu.SemaphoreType.DMA((4, 2)),
        ],
        input_output_aliases={6: 0, 7: 1},
        compiler_params=params(12),
        name="finish_edges",
    )(diffusivity, part, across, inside, from_across, from_inside, new_state, new_section)
    return new_state.reshape(state.shape), new_section.reshape(section.shape)


def solution(mesh):
    field = P("grid", None, None, "colat", "lon")
    placed = (field, field, P(), P(), P("grid", "colat", "lon", None), P("grid", "colat", "lon", None, None))
    return jax.shard_map(
        local, mesh=mesh, in_specs=placed, out_specs=(field, field), check_vma=False
    )
```
